512 devices in a mesh: rep: 32 (over z_lo, x, core), fsdp: 16 (over z_hi, y).
Axes of the slice: x: 4, y: 8, z: 8 (z_hi: 2, z_lo: 4; z = z_hi * 4 + z_lo), core: 2. Of those that a mesh axis runs over, the one named last changes fastest.
Arguments:
- inputs: bfloat16 [32, 8192, 2048], P('rep', 'fsdp'), may hold values from -6 to 6
- key_grads: bfloat16 [32, 8192, 512], P('rep', 'fsdp'), may hold values from -0.08984375 to 0.08984375
- token_ids: int32 [32, 8192], P('rep', 'fsdp'), may hold values from 0 to 128255, as said below
- step: int32 [], replicated, may hold values from 0 to 7
- master: float32 [32, 2048, 512], P('rep', 'fsdp'), may hold values from -0.125 to 0.125
- first_moment: float32 [32, 2048, 512], P('rep', 'fsdp'), may hold values from -3 to 3
- second_moment: float32 [32, 2048, 512], P('rep', 'fsdp'), may hold values from 0.1 to 4
Outputs:
- mixed_master: float32 [32, 2048, 512], P('rep', 'fsdp')
- new_first: float32 [32, 2048, 512], P('rep', 'fsdp')
- new_second: float32 [32, 2048, 512], P('rep', 'fsdp')
- new_keys: bfloat16 [32, 8192, 512], P('rep', 'fsdp')
The draws below stay inside these ranges and needn't reach their ends.
Inputs may be any that keep to these rules, and one draw needn't show every extreme that they name: `token_ids`: 0 marks a padding token; other ids are ordinary tokens.
All inputs are finite; a program needn't handle non-finite values.
Results may differ from the reference program's by a relative error of at most 0.013.
Values may be sent and summed in bfloat16 or wider, within the bound.
A program may use at most 64 MiB of HBM per device.

```python
import math
import jax
import jax.numpy as jnp
from jax import lax

DW = 2048
KW = 512
VOCAB = 128256
TOK_DEV = 512
TOKENS = 8192
REPLICAS = 32
BITS = 4
N_FSDP = 16


def draw_token_ids(key, part):
    key = jax.random.fold_in(key, 11)
    key_ids, key_pad = jax.random.split(key)
    drawn = jax.random.randint(key_ids, (REPLICAS, TOKENS), 1, VOCAB)
    padding = jax.random.randint(key_pad, (REPLICAS, TOKENS), 0, 4)
    return jnp.where(padding == 0, 0, drawn).astype(jnp.int32)


def with_spikes(drawn, own_key, source, target, parts, factor):
    owner, partner = [(jnp.arange(drawn.shape[axis_at]) // (drawn.shape[axis_at] // parts)).reshape([-1 if axis == axis_at else 1 for axis in range(drawn.ndim)]) for axis_at in (source, target)]
    chosen = jax.random.permutation(own_key, parts)[partner]
    strong = (owner == chosen) | (owner == (partner + parts // 2) % parts)
    return jnp.where(strong, factor * drawn, drawn)


def block_scale(own_key, shape, shards, low, top_value):
    level, own = 1.0, jax.random.fold_in(own_key, 6)
    for position, parts in shards:
        heights = jnp.exp(jax.random.uniform(jax.random.fold_in(own, position), (parts,), jnp.float32, low / len(shards), top_value / len(shards)))
        level = level * jnp.repeat(heights, shape[position] // parts).reshape([-1 if axis == position else 1 for axis in range(len(shape))])
    return level


def scatter_about(rng, dims, scale, reach, pieces=(), kind=jnp.bfloat16):
    loudness = block_scale(rng, dims, pieces, -0.22, 0.18) if pieces else 1.0
    array = jax.random.normal(rng, dims, jnp.float32) * scale * loudness
    return jnp.minimum(jnp.maximum(array, -reach), reach).astype(kind)


def noise_with(key, shape, spread, limit, shards, heavy, kind=jnp.bfloat16):
    entries = spread * jax.random.normal(key, shape, jnp.float32)
    if shards:
        entries = entries * block_scale(key, shape, shards, -0.22, 0.18)
    return jnp.clip(with_spikes(entries, jax.random.fold_in(key, 3), *heavy), -limit, limit).astype(kind)


def setup_inputs(seed: int = 0) -> dict:
    streams_of = jax.random.split(jax.random.key(seed), 8)
    inputs = noise_with(streams_of[0], (REPLICAS, TOKENS, DW), 1.0, 6.0, ((0, 32), (1, 16)), (1, 2, 16, 2.0))
    key_grads = scatter_about(streams_of[1], (REPLICAS, TOKENS, KW), 0.015625, 0.08984375, ((0, 32), (1, 16)))
    token_ids = draw_token_ids(jax.random.fold_in(streams_of[7], 71), 0)
    step = jax.random.randint(streams_of[3], (), 0, 8).astype(jnp.int32)
    master = scatter_about(streams_of[4], (REPLICAS, DW, KW), DW ** -0.5, 0.125, ((0, 32), (1, 16)), jnp.float32)
    first_moment = scatter_about(streams_of[5], (REPLICAS, DW, KW), 0.5, 3.0, ((0, 32), (1, 16)), jnp.float32)
    second_moment = jnp.clip(jnp.exp(math.log(4.0) - 3.6888794 * jax.random.uniform(streams_of[6], (REPLICAS, DW, KW), jnp.float32) ** block_scale(streams_of[6], (REPLICAS, DW, KW), ((0, 32), (1, 16)), -0.2, 0.2)), 0.1, 4.0)
    return dict(inputs=inputs, key_grads=key_grads, token_ids=token_ids, step=step, master=master, first_moment=first_moment, second_moment=second_moment)


def adam_step(weights, moment_one, moment_two, gradient, step):
    new_one = 0.9 * moment_one + 0.1 * gradient
    new_two = 0.95 * moment_two + 0.05 * gradient * gradient
    power = (step + 1).astype(jnp.float32)
    corr_one = 1.0 - jnp.power(jnp.float32(0.9), power)
    corr_two = 1.0 - jnp.power(jnp.float32(0.95), power)
    updated = weights - 0.01 * (new_one / corr_one) / (jnp.sqrt(new_two / corr_two) + 1e-08)
    return (updated, new_one, new_two)

def reference(inputs, key_grads, token_ids, step, master, first_moment, second_moment):
    live_rows = (token_ids != 0)[..., None]
    masked_grads = jnp.where(live_rows, key_grads, jnp.zeros_like(key_grads))

    def replica_grad(pair):
        features, cotangent = pair
        feat_blocks = features.reshape(N_FSDP, TOK_DEV, DW)
        cot_blocks = cotangent.reshape(N_FSDP, TOK_DEV, KW)

        def add_block(running, block_pair):
            feat_one, cot_one = block_pair
            part = lax.dot_general(feat_one, cot_one, (((0,), (0,)), ((), ())), preferred_element_type=jnp.float32)
            return (running + part.astype(jnp.bfloat16).astype(jnp.float32), None)
        running, unused = lax.scan(add_block, jnp.zeros((DW, KW), jnp.float32), (feat_blocks, cot_blocks))
        return running
    gradient = lax.map(replica_grad, (inputs, masked_grads))
    updated, new_first, new_second = adam_step(master, first_moment, second_moment, gradient, step)
    bit_number = step % BITS
    partner = jnp.bitwise_xor(jnp.arange(REPLICAS, dtype=jnp.int32), jnp.left_shift(jnp.int32(1), bit_number).astype(jnp.int32))
    mixed_master = 0.5 * (updated + updated[partner])
    params = mixed_master.astype(jnp.bfloat16)

    def replica_keys(pair):
        features, weights = pair
        return jnp.dot(features, weights, preferred_element_type=jnp.float32).astype(jnp.bfloat16)
    new_keys = lax.map(replica_keys, (inputs, params))
    return (mixed_master, new_first, new_second, new_keys)
```

```python
import functools
import math

import jax
import jax.numpy as jnp
from jax import lax
from jax.experimental import pallas as pl
from jax.experimental.pallas import tpu as pltpu
from jax.sharding import PartitionSpec as P

MESH = pl.DeviceIdType.MESH
F32, BF16 = jnp.float32, jnp.bfloat16

NY = 8
NC = 2
OWN, OTHER = 0, 1
CW, CCW = 0, 1
PARTNERS = (1, 2, 4, 8)


def kernel(
    inputs, grads, ids, step, master, first, second,
    mixed_out, first_out, second_out, keys_out,
    x, g, idv, gt, part, rs_in, weights, total, keys, z_send, z_in, mate_send, mate_in,
    w_v, m_v, s_v, mixed_v, first_v, second_v,
    load_sem, rs_ssem, rs_rsem, ag_ssem, ag_rsem, z_ssem, z_rsem, mate_ssem, mate_rsem, gz_ssem, gz_rsem, out_sem,
):
    depth = w_v.shape[0]
    width = w_v.shape[1] // NC
    r, f = lax.axis_index("rep"), lax.axis_index("fsdp")
    y, z = lax.rem(f, NY), f // NY

    def at_y(d):
        return (r, z * NY + lax.rem(y + d + NY, NY))

    across = (r, (1 - z) * NY + y)

    def mate(mask):
        return (r + mask - 2 * mask * lax.rem(r // mask, 2), f)

    towards = (at_y(1), at_y(-1))

    loads = {}

    def load(name, source, target):
        loads[name] = pltpu.make_async_copy(source, target, load_sem.at[len(loads)])
        loads[name].start()

    load("g", grads.at[0], g)
    load("ids", ids, idv)
    order = (4, 3, -3, 2, -2, 1, -1, 0)
    for d in order:
        for zz in (OWN, OTHER):
            plane = z if zz == OWN else 1 - z
            column = pl.multiple_of((plane * NY + lax.rem(y + d + NY, NY)) * depth, depth)
            load((d, zz), inputs.at[0, :, pl.ds(column, depth)], x.at[d % NY, :, pl.ds(zz * depth, depth)])
    load("w", master.at[0], w_v)
    load("m", first.at[0], m_v)
    load("s", second.at[0], s_v)

    barrier = pltpu.get_barrier_semaphore()
    peers = [*towards, across, *[mate(mask) for mask in PARTNERS]]
    for peer in peers:
        pl.semaphore_signal(barrier, inc=1, device_id=peer, device_id_type=MESH)

    loads["g"].wait()
    loads["ids"].wait()
    live = (idv[...] != 0).astype(F32)
    gt[...] = (g[...].astype(F32).T * live).astype(BF16)

    sent = []

    def send(source, target, ssem, rsem, device):
        copy = pltpu.make_async_remote_copy(source, target, ssem, rsem, device_id=device, device_id_type=MESH)
        copy.start()
        sent.append(copy)

    def arrived(target, rsem):
        pltpu.make_async_copy(target, target, rsem).wait()

    def partial(d):
        loads[d, OWN].wait()
        loads[d, OTHER].wait()
        product = jnp.dot(gt[...], x[d % NY], preferred_element_type=F32).astype(BF16)
        part[d % NY, OWN] = product[:, :depth]
        part[d % NY, OTHER] = product[:, depth:]

    def piece(d, zz, c):
        return part.at[d % NY, zz, pl.ds(c * width, width)]

    def far_half(way):
        return OTHER if way == CW else OWN

    def rs_step(c, s, zz):
        for way in (CW, CCW):
            if s == 0 and zz != far_half(way):
                continue
            d = (4 - s) if way == CW else (s - 4)
            own = piece(d, zz, c)
            if s > 1 or (s == 1 and zz == far_half(way)):
                arrived(rs_in.at[way, s - 1, zz, c], rs_rsem.at[way, s - 1, zz, c])
                own[...] = (own[...].astype(F32) + rs_in[way, s - 1, zz, c].astype(F32)).astype(BF16)
            send(own, rs_in.at[way, s, zz, c], rs_ssem.at[way, s, zz, c], rs_rsem.at[way, s, zz, c], towards[way])

    def rs_sum(c, zz):
        own = piece(0, zz, c)[...].astype(F32)
        for way in (CW, CCW):
            arrived(rs_in.at[way, 3, zz, c], rs_rsem.at[way, 3, zz, c])
            own = own + rs_in[way, 3, zz, c].astype(F32)
        return own

    def rs_across(c):
        z_send[c] = rs_sum(c, OTHER).astype(BF16)
        send(z_send.at[c], z_in.at[c], z_ssem.at[c], z_rsem.at[c], across)

    def adam(c):
        if c == 0:
            loads["w"].wait()
            loads["m"].wait()
            loads["s"].wait()
        columns = pl.ds(c * width, width)
        own = rs_sum(c, OWN)
        arrived(z_in.at[c], z_rsem.at[c])
        gradient = (own + z_in[c].astype(F32)).T
        new_one = 0.9 * m_v[:, columns] + 0.1 * gradient
        new_two = 0.95 * s_v[:, columns] + 0.05 * gradient * gradient
        power = jnp.full(new_one.shape, step[0] + 1, jnp.int32).astype(F32)
        corr_one = 1.0 - jnp.exp(power * math.log(0.9))
        corr_two = 1.0 - jnp.exp(power * math.log(0.95))
        updated = w_v[:, columns] - 0.01 * (new_one / corr_one) / (jnp.sqrt(new_two / corr_two) + 1e-08)
        mixed_v[:, columns] = updated
        mate_send[c] = updated.astype(BF16)
        for i, mask in enumerate(PARTNERS):
            send(mate_send.at[c], mate_in.at[c, i], mate_ssem.at[c, i], mate_rsem.at[c, i], mate(mask))
        first_v[:, columns] = new_one
        second_v[:, columns] = new_two

    def mix(c):
        columns = pl.ds(c * width, width)
        bit = jnp.full((depth, width), lax.rem(step[0], len(PARTNERS)), jnp.int32)
        theirs = jnp.zeros((depth, width), F32)
        for i in range(len(PARTNERS)):
            arrived(mate_in.at[c, i], mate_rsem.at[c, i])
            theirs = jnp.where(bit == i, mate_in[c, i].astype(F32), theirs)
        mixed = 0.5 * (mixed_v[:, columns] + theirs)
        mixed_v[:, columns] = mixed
        weights[0, c, :depth] = mixed.astype(BF16)
        send(weights.at[0, c, pl.ds(0, depth)], weights.at[0, c, pl.ds(depth, depth)], gz_ssem.at[c], gz_rsem.at[c], across)

    def ag_step(c, s, zz):
        rows = pl.ds(zz * depth, depth)
        for way in (CW, CCW):
            if s == 4 and zz == far_half(way):
                continue
            have = (1 - s) if way == CW else (s - 1)
            if s > 1:
                arrived(weights.at[have % NY, c, rows], ag_rsem.at[way, s - 1, zz, c])
            elif zz == OTHER and way == CW:
                arrived(weights.at[0, c, rows], gz_rsem.at[c])
            there = -s if way == CW else s
            send(weights.at[have % NY, c, rows], weights.at[there % NY, c, rows], ag_ssem.at[way, s, zz, c], ag_rsem.at[way, s, zz, c], towards[way])

    def ag_last(c):
        arrived(weights.at[4, c, pl.ds(OWN * depth, depth)], ag_rsem.at[CW, 4, OWN, c])
        arrived(weights.at[4, c, pl.ds(OTHER * depth, depth)], ag_rsem.at[CCW, 4, OTHER, c])

    def multiply(c, d):
        term = jnp.dot(x[d % NY], weights[d % NY, c], preferred_element_type=F32)
        if d == 0:
            total[c] = term
        else:
            total[c] += term

    outs = []

    def store(source, target):
        copy = pltpu.make_async_copy(source, target, out_sem.at[len(outs)])
        copy.start()
        outs.append(copy)

    partial(4)
    pl.semaphore_wait(barrier, len(peers))
    rs_step(0, 0, OTHER)
    rs_step(0, 0, OWN)
    partial(3)
    partial(-3)
    rs_step(0, 1, OTHER)
    rs_step(0, 1, OWN)
    rs_step(1, 0, OTHER)
    rs_step(1, 0, OWN)
    partial(2)
    partial(-2)
    rs_step(0, 2, OTHER)
    rs_step(0, 2, OWN)
    partial(1)
    partial(-1)
    partial(0)
    rs_step(0, 3, OTHER)
    rs_step(0, 3, OWN)
    rs_step(1, 1, OTHER)
    rs_step(1, 1, OWN)
    rs_across(0)
    rs_step(1, 2, OTHER)
    rs_step(1, 2, OWN)
    adam(0)
    rs_step(1, 3, OTHER)
    rs_step(1, 3, OWN)
    mix(0)
    ag_step(0, 1, OWN)
    rs_across(1)
    ag_step(0, 1, OTHER)
    ag_step(0, 2, OWN)
    adam(1)
    multiply(0, 0)
    ag_step(0, 2, OTHER)
    multiply(0, 1)
    multiply(0, -1)
    ag_step(0, 3, OWN)
    mix(1)
    ag_step(1, 1, OWN)
    store(mixed_v, mixed_out.at[0])
    store(first_v, first_out.at[0])
    store(second_v, second_out.at[0])
    ag_step(0, 3, OTHER)
    multiply(0, 2)
    multiply(0, -2)
    ag_step(0, 4, OWN)
    ag_step(1, 1, OTHER)
    ag_step(1, 2, OWN)
    multiply(1, 0)
    arrived(weights.at[3, 0, pl.ds(OWN * depth, depth)], ag_rsem.at[CCW, 3, OWN, 0])
    ag_step(0, 4, OTHER)
    arrived(weights.at[-3 % NY, 0, pl.ds(OTHER * depth, depth)], ag_rsem.at[CW, 3, OTHER, 0])
    multiply(0, 3)
    multiply(0, -3)
    ag_step(1, 2, OTHER)
    multiply(1, 1)
    multiply(1, -1)
    ag_step(1, 3, OWN)
    ag_last(0)
    multiply(0, 4)
    keys[:, pl.ds(0, width)] = total[0].astype(BF16)
    store(keys.at[:, pl.ds(0, width)], keys_out.at[0, :, pl.ds(0, width)])
    ag_step(1, 3, OTHER)
    multiply(1, 2)
    multiply(1, -2)
    ag_step(1, 4, OWN)
    arrived(weights.at[3, 1, pl.ds(OWN * depth, depth)], ag_rsem.at[CCW, 3, OWN, 1])
    ag_step(1, 4, OTHER)
    arrived(weights.at[-3 % NY, 1, pl.ds(OTHER * depth, depth)], ag_rsem.at[CW, 3, OTHER, 1])
    multiply(1, 3)
    multiply(1, -3)
    ag_last(1)
    multiply(1, 4)
    keys[:, pl.ds(width, width)] = total[1].astype(BF16)
    store(keys.at[:, pl.ds(width, width)], keys_out.at[0, :, pl.ds(width, width)])

    for copy in sent:
        copy.wait_send()
    for copy in outs:
        copy.wait()


def on_device(inputs, key_grads, token_ids, step, master, first_moment, second_moment):
    tokens, features = inputs.shape[1:]
    depth, columns = master.shape[1:]
    width = columns // NC
    any_space = pl.BlockSpec(memory_space=pl.ANY)
    state = jax.ShapeDtypeStruct(master.shape, F32)
    dma = pltpu.SemaphoreType.DMA
    return pl.pallas_call(
        kernel,
        out_shape=(state, state, state, jax.ShapeDtypeStruct((1, tokens, columns), BF16)),
        in_specs=[any_space] * 3 + [pl.BlockSpec(memory_space=pltpu.SMEM)] + [any_space] * 3,
        out_specs=[any_space] * 4,
        scratch_shapes=[
            pltpu.VMEM((NY, tokens, 2 * depth), BF16),
            pltpu.VMEM((tokens, columns), BF16),
            pltpu.VMEM((1, tokens), jnp.int32),
            pltpu.VMEM((columns, tokens), BF16),
            pltpu.VMEM((NY, 2, columns, depth), BF16),
            pltpu.VMEM((2, 4, 2, NC, width, depth), BF16),
            pltpu.VMEM((NY, NC, 2 * depth, width), BF16),
            pltpu.VMEM((NC, tokens, width), F32),
            pltpu.VMEM((tokens, columns), BF16),
            pltpu.VMEM((NC, width, depth), BF16),
            pltpu.VMEM((NC, width, depth), BF16),
            pltpu.VMEM((NC, depth, width), BF16),
            pltpu.VMEM((NC, len(PARTNERS), depth, width), BF16),
            *[pltpu.VMEM((depth, columns), F32) for _ in range(6)],
            dma((24,)),
            dma((2, 4, 2, NC)),
            dma((2, 4, 2, NC)),
            dma((2, 5, 2, NC)),
            dma((2, 5, 2, NC)),
            dma((NC,)),
            dma((NC,)),
            dma((NC, len(PARTNERS))),
            dma((NC, len(PARTNERS))),
            dma((NC,)),
            dma((NC,)),
            dma((8,)),
        ],
        compiler_params=pltpu.CompilerParams(
            collective_id=0, has_side_effects=True, vmem_limit_bytes=60 * 2**20
        ),
        cost_estimate=pl.CostEstimate(
            flops=4 * tokens * features * columns, bytes_accessed=5 * 2**20, transcendentals=0
        ),
        name="grad_adam_keys",
    )(inputs, key_grads, token_ids, step.reshape(1), master, first_moment, second_moment)


def solution(mesh):
    in_specs = (
        P("rep", "fsdp", None),
        P("rep", "fsdp", None),
        P("rep", "fsdp"),
        P(),
        P("rep", "fsdp", None),
        P("rep", "fsdp", None),
        P("rep", "fsdp", None),
    )
    out_specs = (
        P("rep", "fsdp", None),
        P("rep", "fsdp", None),
        P("rep", "fsdp", None),
        P("rep", "fsdp", None),
    )
    return jax.shard_map(
        on_device, mesh=mesh, in_specs=in_specs, out_specs=out_specs, check_vma=False
    )
```

```python
import functools
import functools
import math

import jax
import jax.numpy as jnp
from jax import lax
from jax.experimental import pallas as pl
from jax.experimental.pallas import tpu as pltpu
from jax.sharding import PartitionSpec as P

MESH = pl.DeviceIdType.MESH
F32, BF16 = jnp.float32, jnp.bfloat16

NY = 8
NC = 4
OWN, OTHER = 0, 1
CW, CCW = 0, 1
PARTNERS = (1, 2, 4, 8)


def kernel(
    masks, inputs, grads, ids, step, master, first, second,
    mixed_v, first_v, second_v, keys,
    x, g, idv, gt, part, rs_in, weights, total, z_send, z_in, mate_send, mate_in, w_v, m_v, s_v,
    load_sem, rs_ssem, rs_rsem, ag_ssem, ag_rsem, z_ssem, z_rsem, mate_ssem, mate_rsem, gz_ssem, gz_rsem,
):
    depth = w_v.shape[0]
    width = w_v.shape[1] // NC
    r, f = lax.axis_index("rep"), lax.axis_index("fsdp")
    y, z = lax.rem(f, NY), f // NY

    def at_y(d):
        return (r, z * NY + lax.rem(y + d + NY, NY))

    across = (r, (1 - z) * NY + y)

    def mate(mask):
        return (r + mask - 2 * mask * lax.rem(r // mask, 2), f)

    towards = (at_y(1), at_y(-1))

    barrier = pltpu.get_barrier_semaphore()
    peers = [*towards, across, *[mate(mask) for mask in masks]]
    for peer in peers:
        pl.semaphore_signal(barrier, inc=1, device_id=peer, device_id_type=MESH)

    loads = {}

    def load(name, source, target):
        loads[name] = pltpu.make_async_copy(source, target, load_sem.at[len(loads)])
        loads[name].start()

    load("g", grads.at[0], g)
    load("ids", ids, idv)
    for d in (4, 3, -3, 2, -2, 1, -1, 0):
        for zz in (OWN, OTHER):
            plane = z if zz == OWN else 1 - z
            column = pl.multiple_of((plane * NY + lax.rem(y + d + NY, NY)) * depth, depth)
            load((d, zz), inputs.at[0, :, pl.ds(column, depth)], x.at[d % NY, :, pl.ds(zz * depth, depth)])
    load("w", master.at[0], w_v)
    load("m", first.at[0], m_v)
    load("s", second.at[0], s_v)

    sent = []

    def send(source, target, ssem, rsem, device):
        copy = pltpu.make_async_remote_copy(source, target, ssem, rsem, device_id=device, device_id_type=MESH)
        copy.start()
        sent.append(copy)

    def arrived(target, rsem):
        pltpu.make_async_copy(target, target, rsem).wait()

    def prepare():
        loads["g"].wait()
        loads["ids"].wait()
        live = (idv[...] != 0).astype(F32)
        gt[...] = (g[...].astype(F32).T * live).astype(BF16)

    def partial(d):
        loads[d, OWN].wait()
        loads[d, OTHER].wait()
        product = jnp.dot(gt[...], x[d % NY], preferred_element_type=F32).astype(BF16)
        part[d % NY, OWN] = product[:, :depth]
        part[d % NY, OTHER] = product[:, depth:]

    def enter():
        pl.semaphore_wait(barrier, len(peers))

    def far_half(way):
        return OTHER if way == CW else OWN

    def rs(s, *pieces):
        for c, zz in pieces:
            for way in (CW, CCW):
                if s == 0 and zz != far_half(way):
                    continue
                d = (4 - s) if way == CW else (s - 4)
                own = part.at[d % NY, zz, pl.ds(c * width, width)]
                if s > 1 or (s == 1 and zz == far_half(way)):
                    arrived(rs_in.at[way, s - 1, zz, c], rs_rsem.at[way, s - 1, zz, c])
                    own[...] = (own[...].astype(F32) + rs_in[way, s - 1, zz, c].astype(F32)).astype(BF16)
                send(own, rs_in.at[way, s, zz, c], rs_ssem.at[way, s, zz, c], rs_rsem.at[way, s, zz, c], towards[way])

    def rs_sum(c, zz):
        own = part[0, zz, pl.ds(c * width, width)].astype(F32)
        for way in (CW, CCW):
            arrived(rs_in.at[way, 3, zz, c], rs_rsem.at[way, 3, zz, c])
            own = own + rs_in[way, 3, zz, c].astype(F32)
        return own

    def rs_across(c):
        z_send[c] = rs_sum(c, OTHER).astype(BF16)
        send(z_send.at[c], z_in.at[c], z_ssem.at[c], z_rsem.at[c], across)

    def adam(c):
        if c == 0:
            loads["w"].wait()
            loads["m"].wait()
            loads["s"].wait()
        columns = pl.ds(c * width, width)
        own = rs_sum(c, OWN)
        arrived(z_in.at[c], z_rsem.at[c])
        gradient = (own + z_in[c].astype(F32)).T
        new_one = 0.9 * m_v[:, columns] + 0.1 * gradient
        new_two = 0.95 * s_v[:, columns] + 0.05 * gradient * gradient
        power = jnp.full(new_one.shape, step[0] + 1, jnp.int32).astype(F32)
        corr_one = 1.0 - jnp.exp(power * math.log(0.9))
        corr_two = 1.0 - jnp.exp(power * math.log(0.95))
        updated = w_v[:, columns] - 0.01 * (new_one / corr_one) / (jnp.sqrt(new_two / corr_two) + 1e-08)
        mate_send[c] = updated.astype(BF16)
        for i, mask in enumerate(masks):
            send(mate_send.at[c], mate_in.at[c, i], mate_ssem.at[c, i], mate_rsem.at[c, i], mate(mask))
        w_v[:, columns] = updated
        first_v[0, :, columns] = new_one
        second_v[0, :, columns] = new_two

    def block(d, c, zz):
        return weights.at[d % NY, c // 2, pl.ds(zz * depth, depth), pl.ds((c % 2) * width, width)]

    def mix(c):
        columns = pl.ds(c * width, width)
        bit = jnp.full((depth, width), lax.rem(step[0], len(PARTNERS)), jnp.int32)
        theirs = None
        for i, mask in enumerate(masks):
            arrived(mate_in.at[c, i], mate_rsem.at[c, i])
            one = mate_in[c, i].astype(F32)
            theirs = one if theirs is None else jnp.where(bit == PARTNERS.index(mask), one, theirs)
        mixed = 0.5 * (w_v[:, columns] + theirs)
        mixed_v[0, :, columns] = mixed
        block(0, c, OWN)[...] = mixed.astype(BF16)
        send(block(0, c, OWN), block(0, c, OTHER), gz_ssem.at[c], gz_rsem.at[c], across)

    def ag(s, *pieces):
        for c, zz in pieces:
            for way in (CW, CCW):
                if s == 4 and zz == far_half(way):
                    continue
                have = (1 - s) if way == CW else (s - 1)
                if s > 1:
                    ag_wait(way, s - 1, c, zz)
                elif zz == OTHER and way == CW:
                    arrived(block(0, c, OTHER), gz_rsem.at[c])
                there = -s if way == CW else s
                send(block(have, c, zz), block(there, c, zz), ag_ssem.at[way, s, zz, c], ag_rsem.at[way, s, zz, c], towards[way])

    waited = set()

    def ag_wait(way, s, c, zz):
        if (way, s, c, zz) not in waited:
            waited.add((way, s, c, zz))
            arrived(block(-s if way == CW else s, c, zz), ag_rsem.at[way, s, zz, c])

    def multiply(pair, *ds):
        for d in ds:
            for c in (2 * pair, 2 * pair + 1):
                for zz in (OWN, OTHER):
                    if d == 4:
                        ag_wait(CW if zz == OWN else CCW, 4, c, zz)
                    elif d != 0:
                        ag_wait(CW if d < 0 else CCW, abs(d), c, zz)
            term = jnp.dot(x[d % NY], weights[d % NY, pair], preferred_element_type=F32)
            if d == 0:
                total[pair] = term
            elif d != 4:
                total[pair] += term
            else:
                keys[0, :, pl.ds(pair * 2 * width, 2 * width)] = (total[pair] + term).astype(BF16)

    w0, o0, w1, o1 = (0, OWN), (0, OTHER), (1, OWN), (1, OTHER)
    w2, o2, w3, o3 = (2, OWN), (2, OTHER), (3, OWN), (3, OTHER)

    prepare()
    partial(4)
    enter()
    rs(0, o0, w0, o1, w1)
    partial(3)
    partial(-3)
    rs(0, o2, w2, o3, w3)
    partial(2)
    partial(-2)
    rs(1, o0, o1, w0, w1)
    partial(1)
    partial(-1)
    partial(0)
    rs(1, o2, o3)
    rs(2, o0, o1, w0, w1)
    rs(1, w2, w3)
    rs(2, o2, o3)
    rs(3, o0, o1, w0, w1)
    rs(2, w2, w3)
    rs_across(0)
    rs_across(1)
    rs(3, o2, o3)
    rs(3, w2, w3)
    adam(0)
    adam(1)
    rs_across(2)
    rs_across(3)
    mix(0)
    ag(1, w0)
    mix(1)
    ag(1, w1)
    adam(2)
    adam(3)
    ag(2, w0, w1)
    ag(1, o0, o1)
    multiply(0, 0)
    mix(2)
    ag(1, w2)
    mix(3)
    ag(1, w3)
    ag(3, w0, w1)
    ag(2, o0, o1)
    multiply(0, 1, -1)
    ag(2, w2, w3)
    ag(4, w0, w1)
    ag(1, o2, o3)
    multiply(1, 0)
    ag(3, o0, o1)
    multiply(0, 2, -2)
    ag(3, w2, w3)
    ag(2, o2, o3)
    multiply(1, 1, -1)
    ag(4, o0, o1)
    multiply(0, 3, -3)
    ag(4, w2, w3)
    ag(3, o2, o3)
    multiply(1, 2, -2)
    multiply(0, 4)
    ag(4, o2, o3)
    multiply(1, 3, -3, 4)
    for copy in sent:
        copy.wait_send()


def store(*refs):
    count = len(refs) // 2
    sem = refs[-1]
    copies = [pltpu.make_async_copy(refs[i], refs[count + i], sem.at[i]) for i in range(count)]
    for copy in copies:
        copy.start()
    for copy in copies:
        copy.wait()


def on_device(inputs, key_grads, token_ids, step, master, first_moment, second_moment):
    tokens, features = inputs.shape[1:]
    depth, columns = master.shape[1:]
    width = columns // NC
    hbm = pl.BlockSpec(memory_space=pltpu.HBM)
    vmem = pl.BlockSpec(memory_space=pltpu.VMEM)
    dma = pltpu.SemaphoreType.DMA
    shapes = [(master.shape, F32)] * 3 + [((1, tokens, columns), BF16)]

    def with_partner(bit, *operands):
        masks = (PARTNERS[bit],)
        results = pl.pallas_call(
            functools.partial(kernel, masks),
            out_shape=[pltpu.VMEM(shape, dtype) for shape, dtype in shapes],
            in_specs=[hbm] * 3 + [pl.BlockSpec(memory_space=pltpu.SMEM)] + [hbm] * 3,
            out_specs=[vmem] * 4,
            scratch_shapes=[
                pltpu.VMEM((NY, tokens, 2 * depth), BF16),
                pltpu.VMEM((tokens, columns), BF16),
                pltpu.VMEM((1, tokens), jnp.int32),
                pltpu.VMEM((columns, tokens), BF16),
                pltpu.VMEM((NY, 2, columns, depth), BF16),
                pltpu.VMEM((2, 4, 2, NC, width, depth), BF16),
                pltpu.VMEM((NY, NC // 2, 2 * depth, 2 * width), BF16),
                pltpu.VMEM((NC // 2, tokens, 2 * width), F32),
                pltpu.VMEM((NC, width, depth), BF16),
                pltpu.VMEM((NC, width, depth), BF16),
                pltpu.VMEM((NC, depth, width), BF16),
                pltpu.VMEM((NC, len(masks), depth, width), BF16),
                *[pltpu.VMEM((depth, columns), F32) for _ in range(3)],
                dma((24,)),
                dma((2, 4, 2, NC)),
                dma((2, 4, 2, NC)),
                dma((2, 5, 2, NC)),
                dma((2, 5, 2, NC)),
                dma((NC,)),
                dma((NC,)),
                dma((NC, len(masks))),
                dma((NC, len(masks))),
                dma((NC,)),
                dma((NC,)),
            ],
            compiler_params=pltpu.CompilerParams(
                collective_id=bit, has_side_effects=True, vmem_limit_bytes=58 * 2**20
            ),
            cost_estimate=pl.CostEstimate(
                flops=4 * tokens * features * columns, bytes_accessed=5 * 2**20, transcendentals=0
            ),
            name="grad_adam_keys",
        )(*operands)
        return pl.pallas_call(
            store,
            out_shape=[jax.ShapeDtypeStruct(shape, dtype) for shape, dtype in shapes],
            in_specs=[vmem] * 4,
            out_specs=[hbm] * 4,
            scratch_shapes=[dma((4,))],
            name="store_results",
        )(*results)

    branches = [functools.partial(with_partner, bit) for bit in range(len(PARTNERS))]
    return lax.switch(
        lax.rem(step, len(PARTNERS)), branches,
        inputs, key_grads, token_ids, step.reshape(1), master, first_moment, second_moment,
    )


def solution(mesh):
    in_specs = (
        P("rep", "fsdp", None),
        P("rep", "fsdp", None),
        P("rep", "fsdp"),
        P(),
        P("rep", "fsdp", None),
        P("rep", "fsdp", None),
        P("rep", "fsdp", None),
    )
    out_specs = (
        P("rep", "fsdp", None),
        P("rep", "fsdp", None),
        P("rep", "fsdp", None),
        P("rep", "fsdp", None),
    )
    return jax.shard_map(
        on_device, mesh=mesh, in_specs=in_specs, out_specs=out_specs, check_vma=False
    )
```

```python
import functools
import functools
import math

import jax
import jax.numpy as jnp
from jax import lax
from jax.experimental import pallas as pl
from jax.experimental.pallas import tpu as pltpu
from jax.sharding import PartitionSpec as P

MESH = pl.DeviceIdType.MESH
F32, BF16 = jnp.float32, jnp.bfloat16

NY = 8
NC = 4
OWN, OTHER = 0, 1
CW, CCW = 0, 1
PARTNERS = (1, 2, 4, 8)
SHARED = ((0, 1), (0,), (0,), (0,))


def kernel(
    mask, shared, inputs, grads, ids, step, master, first, second,
    mixed_v, first_v, second_v, keys,
    x, g, idv, gt, part, rs_in, zf_in, weights, total, z_send, z_in, mate_send, mate_in, w_v, m_v, s_v,
    load_sem, rs_ssem, rs_rsem, ag_ssem, ag_rsem, z_ssem, z_rsem, mate_ssem, mate_rsem, gz_ssem, gz_rsem, zf_ssem, zf_rsem, fwd_ssem, fwd_rsem,
):
    depth = w_v.shape[0]
    width = w_v.shape[1] // NC
    r, f = lax.axis_index("rep"), lax.axis_index("fsdp")
    y, z = lax.rem(f, NY), f // NY

    def at_y(d):
        return (r, z * NY + lax.rem(y + d + NY, NY))

    across = (r, (1 - z) * NY + y)

    def mate(mask):
        return (r + mask - 2 * mask * lax.rem(r // mask, 2), f)

    towards = (at_y(1), at_y(-1))

    barrier = pltpu.get_barrier_semaphore()
    peers = [*towards, across, mate(mask)]
    for peer in peers:
        pl.semaphore_signal(barrier, inc=1, device_id=peer, device_id_type=MESH)

    loads = {}

    def load(name, source, target):
        loads[name] = pltpu.make_async_copy(source, target, load_sem.at[len(loads)])
        loads[name].start()

    load("g", grads.at[0], g)
    load("ids", ids, idv)
    for d in (4, 3, -3, 2, -2, 1, -1, 0):
        for zz in (OWN, OTHER):
            plane = z if zz == OWN else 1 - z
            column = pl.multiple_of((plane * NY + lax.rem(y + d + NY, NY)) * depth, depth)
            load((d, zz), inputs.at[0, :, pl.ds(column, depth)], x.at[d % NY, :, pl.ds(zz * depth, depth)])
    load("w", master.at[0], w_v)
    load("m", first.at[0], m_v)
    load("s", second.at[0], s_v)

    sent = []

    def send(source, target, ssem, rsem, device):
        copy = pltpu.make_async_remote_copy(source, target, ssem, rsem, device_id=device, device_id_type=MESH)
        copy.start()
        sent.append(copy)

    def arrived(target, rsem):
        pltpu.make_async_copy(target, target, rsem).wait()

    def prepare():
        loads["g"].wait()
        loads["ids"].wait()
        live = (idv[...] != 0).astype(F32)
        gt[...] = (g[...].astype(F32).T * live).astype(BF16)

    def partial(d):
        loads[d, OWN].wait()
        loads[d, OTHER].wait()
        product = jnp.dot(gt[...], x[d % NY], preferred_element_type=F32).astype(BF16)
        part[d % NY, OWN] = product[:, :depth]
        part[d % NY, OTHER] = product[:, depth:]

    def enter():
        pl.semaphore_wait(barrier, len(peers))

    def far_half(way):
        return OTHER if way == CW else OWN

    def rs(s, *pieces):
        for c, zz in pieces:
            for way in (CW, CCW):
                if s == 0 and zz != far_half(way):
                    continue
                d = (4 - s) if way == CW else (s - 4)
                own = part.at[d % NY, zz, pl.ds(c * width, width)]
                if s > 1 or (s == 1 and zz == far_half(way)):
                    arrived(rs_in.at[way, s - 1, zz, c], rs_rsem.at[way, s - 1, zz, c])
                    own[...] = (own[...].astype(F32) + rs_in[way, s - 1, zz, c].astype(F32)).astype(BF16)
                send(own, rs_in.at[way, s, zz, c], rs_ssem.at[way, s, zz, c], rs_rsem.at[way, s, zz, c], towards[way])

    def rs_sum(c, zz):
        own = part[0, zz, pl.ds(c * width, width)].astype(F32)
        for way in (CW, CCW):
            arrived(rs_in.at[way, 3, zz, c], rs_rsem.at[way, 3, zz, c])
            own = own + rs_in[way, 3, zz, c].astype(F32)
        return own

    def rs_across(c):
        z_send[c] = rs_sum(c, OTHER).astype(BF16)
        send(z_send.at[c], z_in.at[c], z_ssem.at[c], z_rsem.at[c], across)

    last = NC - 1
    half = width // 2

    def last_piece(d):
        return part.at[d % NY, OWN, pl.ds(last * width, width)]

    def zf_send(d):
        send(part.at[d % NY, OTHER, pl.ds(last * width, width)], zf_in.at[d % NY], zf_ssem.at[d % NY], zf_rsem.at[d % NY], across)

    def zf_add(d):
        arrived(zf_in.at[d % NY], zf_rsem.at[d % NY])
        own = last_piece(d)
        own[...] = (own[...].astype(F32) + zf_in[d % NY].astype(F32)).astype(BF16)

    def zf_rs(s):
        for d in (4,) if s == 0 else (4 - s, s - 4):
            zf_add(d)
        for way in (CW, CCW):
            d = (4 - s) if way == CW else (s - 4)
            inbox, ssem, rsem = rs_in.at[way, :, OWN, last], rs_ssem.at[way, :, OWN, last], rs_rsem.at[way, :, OWN, last]
            halved = pl.ds(way * half, half)
            whole = pl.ds(0, width)
            if s > 0:
                rows = halved if s == 1 else whole
                arrived(inbox.at[s - 1, rows], rsem.at[s - 1])
                own = last_piece(d).at[rows]
                own[...] = (own[...].astype(F32) + inbox[s - 1, rows].astype(F32)).astype(BF16)
            rows = halved if s == 0 else whole
            send(last_piece(d).at[rows], inbox.at[s, rows], ssem.at[s], rsem.at[s], towards[way])

    def adam(c):
        for name in ("w", "m", "s"):
            if name in loads:
                loads.pop(name).wait()
        columns = pl.ds(c * width, width)
        if c == last:
            zf_add(0)
        own = rs_sum(c, OWN)
        if c != last:
            arrived(z_in.at[c], z_rsem.at[c])
            own = own + z_in[c].astype(F32)
        gradient = own.T
        new_one = 0.9 * m_v[:, columns] + 0.1 * gradient
        new_two = 0.95 * s_v[:, columns] + 0.05 * gradient * gradient
        power = jnp.full(new_one.shape, step[0] + 1, jnp.int32).astype(F32)
        corr_one = 1.0 - jnp.exp(power * math.log(0.9))
        corr_two = 1.0 - jnp.exp(power * math.log(0.95))
        updated = w_v[:, columns] - 0.01 * (new_one / corr_one) / (jnp.sqrt(new_two / corr_two) + 1e-08)
        mate_send[c] = updated.astype(BF16)
        send(mate_send.at[c], mate_in.at[c], mate_ssem.at[c], mate_rsem.at[c], mate(mask))
        w_v[:, columns] = updated
        first_v[0, :, columns] = new_one
        second_v[0, :, columns] = new_two

    mine = lax.rem(r // mask, 2)

    def columns_of(c):
        if c // 2 in shared:
            return pl.ds(pl.multiple_of(lax.rem(mine + c, 2) * width, width), width)
        return pl.ds((c % 2) * width, width)

    def block(d, c, zz):
        return weights.at[d % NY, c // 2, pl.ds(zz * depth, depth), columns_of(c)]

    def mix(c):
        columns = pl.ds(c * width, width)
        arrived(mate_in.at[c], mate_rsem.at[c])
        mixed = 0.5 * (w_v[:, columns] + mate_in[c].astype(F32))
        mixed_v[0, :, columns] = mixed
        weights[0, c // 2, :depth, pl.ds((c % 2) * width, width)] = mixed.astype(BF16)
        if c // 2 not in shared:
            to_plane(c)

    def to_plane(c):
        send(block(0, c, OWN), block(0, c, OTHER), gz_ssem.at[c], gz_rsem.at[c], across)

    def gz(pair):
        to_plane(2 * pair)

    waited = set()

    def once(key, target, rsem):
        if key not in waited:
            waited.add(key)
            arrived(target, rsem)

    def ag_wait(d, c, zz):
        way, s = (CCW, d) if 0 < d < 4 else (CW, -d)
        if d == 4:
            way, s = (CW if zz == OWN else CCW), 4
        if d != 0:
            once((d, c, zz), block(d, c, zz), ag_rsem.at[way, s, zz, c])
        elif zz == OTHER:
            once((d, c, zz), block(d, c, zz), gz_rsem.at[c])

    def ag(s, *pieces):
        for c, zz in pieces:
            for way in (CW, CCW):
                if s == 4 and zz == far_half(way):
                    continue
                have, there = (1 - s, -s) if way == CW else (s - 1, s)
                ag_wait(have, c, zz)
                send(block(have, c, zz), block(there, c, zz), ag_ssem.at[way, s, zz, c], ag_rsem.at[way, s, zz, c], towards[way])

    def fwd(pair, d, zz):
        c = 2 * pair
        ag_wait(d, c, zz)
        there = block(d, c, zz)
        send(there, there, fwd_ssem.at[pair, d % NY, zz], fwd_rsem.at[pair, d % NY, zz], mate(mask))

    def fwd_wait(pair, d, zz):
        if d != 0 or zz == OTHER:
            arrived(block(d, 2 * pair + 1, zz), fwd_rsem.at[pair, d % NY, zz])

    def multiply(pair, *ds):
        for d in ds:
            for zz in (OWN, OTHER):
                ag_wait(d, 2 * pair, zz)
                if pair in shared:
                    fwd_wait(pair, d, zz)
                else:
                    ag_wait(d, 2 * pair + 1, zz)
            term = jnp.dot(x[d % NY], weights[d % NY, pair], preferred_element_type=F32)
            if d == 0:
                total[pair] = term
            elif d != 4:
                total[pair] += term
            else:
                keys[0, :, pl.ds(pair * 2 * width, 2 * width)] = (total[pair] + term).astype(BF16)

    w0, o0, w1, o1 = (0, OWN), (0, OTHER), (1, OWN), (1, OTHER)
    w2, o2, w3, o3 = (2, OWN), (2, OTHER), (3, OWN), (3, OTHER)

    prepare()
    if 1 in shared:
        partial(4)
        enter()
        rs(0, o1, w1, o0, o2)
        partial(-2)
        partial(-3)
        rs(0, w0, w2)
        zf_send(4)
        zf_send(-3)
        partial(-1)
        partial(3)
        zf_send(3)
        rs(1, o1, w1)
        partial(2)
        rs(1, o0)
        zf_send(2)
        partial(1)
        zf_send(1)
        rs(1, o2, w0, w2)
        partial(0)
        rs(2, o1)
        zf_send(0)
        zf_send(-2)
        zf_send(-1)
        rs(2, w1, o0)
        zf_rs(0)
        rs(2, o2, w0, w2)
        rs(3, o1, w1, o0)
        zf_rs(1)
        rs(3, o2, w0, w2)
        rs_across(1)
        rs_across(0)
        zf_rs(2)
        rs_across(2)
        zf_rs(3)
        adam(1)
        adam(0)
        adam(3)
        adam(2)
        mix(1)
        mix(0)
        gz(0)
        ag(1, w0)
        mix(3)
        mix(2)
        gz(1)
        ag(1, w2)
        ag(2, w0)
        fwd(0, 1, OWN)
        fwd(0, -1, OWN)
        ag(2, w2)
        fwd(1, -1, OWN)
        fwd(1, 1, OWN)
        fwd(0, -2, OWN)
        ag(1, o0)
        ag(3, w0)
        fwd(0, 2, OWN)
        fwd(0, 0, OTHER)
        fwd(1, 2, OWN)
        ag(1, o2)
        ag(3, w2)
        fwd(1, 0, OTHER)
        fwd(1, -2, OWN)
        multiply(0, 0)
        ag(2, o0)
        fwd(0, 1, OTHER)
        fwd(0, -1, OTHER)
        fwd(0, 3, OWN)
        fwd(0, -3, OWN)
        ag(4, w0)
        multiply(1, 0)
        ag(2, o2)
        fwd(1, 1, OTHER)
        fwd(1, -1, OTHER)
        fwd(1, -3, OWN)
        ag(4, w2)
        multiply(0, 1)
        fwd(1, 3, OWN)
        multiply(0, -1)
        fwd(0, -2, OTHER)
        ag(3, o0)
        fwd(0, 2, OTHER)
        fwd(0, 4, OWN)
        multiply(1, 1, -1)
        fwd(1, 2, OTHER)
        ag(3, o2)
        fwd(1, -2, OTHER)
        fwd(1, 4, OWN)
        multiply(0, -2, 2)
        fwd(0, -3, OTHER)
        ag(4, o0)
        fwd(0, 3, OTHER)
        multiply(1, 2, -2)
        ag(4, o2)
        fwd(1, -3, OTHER)
        fwd(1, 3, OTHER)
        multiply(0, -3, 3)
        fwd(0, 4, OTHER)
        multiply(1, -3, 3)
        fwd(1, 4, OTHER)
        multiply(0, 4)
        multiply(1, 4)
    else:
        partial(4)
        enter()
        rs(0, o0)
        zf_send(4)
        rs(0, o1, w0, w2, o2, w1)
        partial(-1)
        zf_send(-1)
        partial(-3)
        zf_send(-3)
        partial(3)
        partial(2)
        rs(1, o0)
        partial(0)
        zf_send(3)
        rs(1, o1, w2)
        partial(1)
        rs(1, o2, w1)
        zf_send(1)
        zf_send(2)
        zf_send(0)
        partial(-2)
        zf_send(-2)
        rs(2, o0)
        zf_rs(0)
        rs(2, o1)
        rs(1, w0)
        rs(2, w2, o2, w1)
        rs(3, o0)
        zf_rs(1)
        rs(3, o1)
        rs(2, w0)
        rs(3, w2, o2, w1)
        rs_across(0)
        rs_across(1)
        zf_rs(2)
        rs(3, w0)
        rs_across(2)
        zf_rs(3)
        adam(0)
        adam(1)
        adam(3)
        mix(0)
        adam(2)
        mix(1)
        gz(0)
        ag(1, w0)
        mix(3)
        ag(1, w3)
        mix(2)
        ag(1, w2)
        ag(2, w0)
        fwd(0, 1, OWN)
        fwd(0, -1, OWN)
        ag(2, w3, w2)
        ag(3, w0)
        fwd(0, 0, OTHER)
        fwd(0, -2, OWN)
        fwd(0, 2, OWN)
        ag(1, o0)
        ag(3, w3)
        ag(1, o3)
        ag(3, w2)
        fwd(0, -3, OWN)
        ag(1, o2)
        multiply(0, 0)
        ag(2, o0)
        fwd(0, 1, OTHER)
        fwd(0, -1, OTHER)
        multiply(1, 0)
        fwd(0, 3, OWN)
        ag(4, w0, w3)
        ag(2, o3)
        ag(4, w2)
        multiply(1, 1)
        multiply(0, 1)
        ag(2, o2)
        multiply(1, -1)
        fwd(0, 2, OTHER)
        ag(3, o0)
        fwd(0, -2, OTHER)
        multiply(0, -1)
        fwd(0, 4, OWN)
        ag(3, o3)
        multiply(1, 2)
        multiply(0, 2)
        fwd(0, 3, OTHER)
        ag(4, o0)
        multiply(0, -2)
        ag(3, o2)
        multiply(1, -2)
        fwd(0, -3, OTHER)
        ag(4, o3)
        multiply(0, 3)
        fwd(0, 4, OTHER)
        multiply(1, -3)
        ag(4, o2)
        multiply(1, 3)
        multiply(0, -3, 4)
        multiply(1, 4)

    for copy in sent:
        copy.wait_send()


def store(*refs):
    count = len(refs) // 2
    sem = refs[-1]
    copies = [pltpu.make_async_copy(refs[i], refs[count + i], sem.at[i]) for i in range(count)]
    for copy in copies:
        copy.start()
    for copy in copies:
        copy.wait()


def on_device(inputs, key_grads, token_ids, step, master, first_moment, second_moment):
    tokens, features = inputs.shape[1:]
    depth, columns = master.shape[1:]
    width = columns // NC
    hbm = pl.BlockSpec(memory_space=pltpu.HBM)
    vmem = pl.BlockSpec(memory_space=pltpu.VMEM)
    any_space = pl.BlockSpec(memory_space=pl.ANY)
    dma = pltpu.SemaphoreType.DMA
    shapes = [(master.shape, F32)] * 3 + [((1, tokens, columns), BF16)]

    def with_partner(bit, *operands):
        mask = PARTNERS[bit]
        shared = SHARED[bit]
        results = pl.pallas_call(
            functools.partial(kernel, mask, shared),
            out_shape=[pltpu.VMEM(shape, dtype) for shape, dtype in shapes],
            in_specs=[hbm] * 3 + [pl.BlockSpec(memory_space=pltpu.SMEM)] + [hbm] * 3,
            out_specs=[vmem] * 4,
            scratch_shapes=[
                pltpu.VMEM((NY, tokens, 2 * depth), BF16),
                pltpu.VMEM((tokens, columns), BF16),
                pltpu.VMEM((1, tokens), jnp.int32),
                pltpu.VMEM((columns, tokens), BF16),
                pltpu.VMEM((NY, 2, columns, depth), BF16),
                pltpu.VMEM((2, 4, 2, NC, width, depth), BF16),
                pltpu.VMEM((NY, width, depth), BF16),
                pltpu.VMEM((NY, NC // 2, 2 * depth, 2 * width), BF16),
                pltpu.VMEM((NC // 2, tokens, 2 * width), F32),
                pltpu.VMEM((NC, width, depth), BF16),
                pltpu.VMEM((NC, width, depth), BF16),
                pltpu.VMEM((NC, depth, width), BF16),
                pltpu.VMEM((NC, depth, width), BF16),
                *[pltpu.VMEM((depth, columns), F32) for _ in range(3)],
                dma((24,)),
                dma((2, 4, 2, NC)),
                dma((2, 4, 2, NC)),
                dma((2, 5, 2, NC)),
                dma((2, 5, 2, NC)),
                dma((NC,)),
                dma((NC,)),
                dma((NC,)),
                dma((NC,)),
                dma((NC,)),
                dma((NC,)),
                dma((NY,)),
                dma((NY,)),
                dma((NC // 2, NY, 2)),
                dma((NC // 2, NY, 2)),
            ],
            compiler_params=pltpu.CompilerParams(
                collective_id=bit, has_side_effects=True, vmem_limit_bytes=58 * 2**20
            ),
            cost_estimate=pl.CostEstimate(
                flops=4 * tokens * features * columns, bytes_accessed=5 * 2**20, transcendentals=0
            ),
            name="grad_adam_keys",
        )(*operands)
        results = [pltpu.with_memory_space_constraint(result, pltpu.VMEM) for result in results]
        return pl.pallas_call(
            store,
            out_shape=[jax.ShapeDtypeStruct(shape, dtype) for shape, dtype in shapes],
            in_specs=[any_space] * 4,
            out_specs=[any_space] * 4,
            scratch_shapes=[dma((4,))],
            name="store_results",
        )(*results)

    branches = [functools.partial(with_partner, bit) for bit in range(len(PARTNERS))]
    return lax.switch(
        lax.rem(step, len(PARTNERS)), branches,
        inputs, key_grads, token_ids, step.reshape(1), master, first_moment, second_moment,
    )


def solution(mesh):
    in_specs = (
        P("rep", "fsdp", None),
        P("rep", "fsdp", None),
        P("rep", "fsdp"),
        P(),
        P("rep", "fsdp", None),
        P("rep", "fsdp", None),
        P("rep", "fsdp", None),
    )
    out_specs = (
        P("rep", "fsdp", None),
        P("rep", "fsdp", None),
        P("rep", "fsdp", None),
        P("rep", "fsdp", None),
    )
    return jax.shard_map(
        on_device, mesh=mesh, in_specs=in_specs, out_specs=out_specs, check_vma=False
    )
```

```python
import functools
import functools
import math

import jax
import jax.numpy as jnp
from jax import lax
from jax.experimental import pallas as pl
from jax.experimental.pallas import tpu as pltpu
from jax.sharding import PartitionSpec as P

MESH = pl.DeviceIdType.MESH
F32, BF16 = jnp.float32, jnp.bfloat16

NY = 8
NC = 4
OWN, OTHER = 0, 1
CW, CCW = 0, 1
PARTNERS = (1, 2, 4, 8)
SHARED = ((0, 1, 2, 3), (0, 1, 2), (0, 1, 2), (0, 1, 2))


def kernel(
    mask, shared, inputs, grads, ids, step, master, first, second,
    mixed_v, first_v, second_v, keys,
    x, g, idv, gt, part, rs_in, zf_in, weights, total, z_send, z_in, mate_send, mate_in, state, count,
    load_sem, send_sem, rs_sem, ag_sem, z_sem, mate_sem, gz_sem, zf_sem, fwd_sem,
):
    w_v, m_v, s_v = state.at[0], state.at[1], state.at[2]
    depth = w_v.shape[0]
    width = w_v.shape[1] // NC
    r, f = lax.axis_index("rep"), lax.axis_index("fsdp")
    y, z = lax.rem(f, NY), f // NY

    def at_y(d):
        return (r, z * NY + lax.rem(y + d + NY, NY))

    across = (r, (1 - z) * NY + y)

    def mate(mask):
        return (r + mask - 2 * mask * lax.rem(r // mask, 2), f)

    towards = (at_y(1), at_y(-1))

    def load(i, source, target):
        pltpu.make_async_copy(source, target, load_sem.at[i]).start()

    def loaded(i, target):
        pltpu.make_async_copy(target, target, load_sem.at[i]).wait()

    def load_inputs(*ds):
        for d in ds:
            for zz in (OWN, OTHER):
                plane = z if zz == OWN else 1 - z
                column = pl.multiple_of((plane * NY + lax.rem(y + d + NY, NY)) * depth, depth)
                load(d % NY, inputs.at[0, :, pl.ds(column, depth)], x.at[d % NY, :, pl.ds(zz * depth, depth)])

    load(NY, grads.at[0], g)
    load(NY + 1, ids, idv)
    load_inputs(4)
    barrier = pltpu.get_barrier_semaphore()
    peers = [*towards, at_y(2), at_y(-2), across, mate(mask)]
    for peer in peers:
        pl.semaphore_signal(barrier, inc=1, device_id=peer, device_id_type=MESH)
    load_inputs(3, -3, 2, -2, 1, -1, 0)
    load(NY + 2, master.at[0], w_v)
    load(NY + 2, first.at[0], m_v)
    load(NY + 2, second.at[0], s_v)

    sent = []
    waited = set()

    def send(source, target, sem, device):
        copy = pltpu.make_async_remote_copy(source, target, send_sem.at[0], sem, device_id=device, device_id_type=MESH)
        copy.start()
        sent.append(math.prod(source.shape) // depth)

    def wait(rows, sem):
        some = count.at[pl.ds(0, rows)]
        pltpu.make_async_copy(some, some, sem).wait()

    def prepare():
        loaded(NY, g)
        loaded(NY + 1, idv)
        live = (idv[...] != 0).astype(F32)
        gt[...] = (g[...].astype(F32).T * live).astype(BF16)

    def partial(d):
        loaded(d % NY, x.at[d % NY])
        product = jnp.dot(gt[...], x[d % NY], preferred_element_type=F32).astype(BF16)
        part[d % NY, OWN] = product[:, :depth]
        part[d % NY, OTHER] = product[:, depth:]

    def enter():
        pl.semaphore_wait(barrier, len(peers))

    def far_half(way):
        return OTHER if way == CW else OWN

    def rs(s, *pieces):
        for c, zz in pieces:
            if s > 0:
                wait(width if s == 1 else 2 * width, rs_sem.at[s - 1, zz, c])
            for way in (CW, CCW):
                if s == 0 and zz != far_half(way):
                    continue
                d = (4 - s) if way == CW else (s - 4)
                own = part.at[d % NY, zz, pl.ds(c * width, width)]
                if s > 1 or (s == 1 and zz == far_half(way)):
                    own[...] = (own[...].astype(F32) + rs_in[way, s - 1, zz, c].astype(F32)).astype(BF16)
                send(own, rs_in.at[way, s, zz, c], rs_sem.at[s, zz, c], towards[way])

    def rs_sum(c, zz):
        own = part[0, zz, pl.ds(c * width, width)].astype(F32)
        for s in (2, 3) if c == NC - 1 else (3,):
            wait(2 * width, rs_sem.at[s, zz, c])
            for way in (CW, CCW):
                own = own + rs_in[way, s, zz, c].astype(F32)
        return own

    def rs_across(c):
        z_send[c] = rs_sum(c, OTHER).astype(BF16)
        send(z_send.at[c], z_in.at[c], z_sem.at[c], across)

    last = NC - 1
    half = width // 2

    def last_piece(d):
        return part.at[d % NY, OWN, pl.ds(last * width, width)]

    def zf_send(d):
        send(part.at[d % NY, OTHER, pl.ds(last * width, width)], zf_in.at[d % NY], zf_sem.at[abs(d)], across)

    def zf_add(*ds):
        wait(len(ds) * width, zf_sem.at[abs(ds[0])])
        for d in ds:
            own = last_piece(d)
            own[...] = (own[...].astype(F32) + zf_in[d % NY].astype(F32)).astype(BF16)

    def zf_rs(s):
        zf_add(*((4,) if s == 0 else (4 - s, s - 4)))
        if s == 2:
            wait(width, rs_sem.at[0, OWN, last])
            wait(2 * width, rs_sem.at[1, OWN, last])
        for way in (CW, CCW):
            d = (4 - s) if way == CW else (s - 4)
            relay = at_y((2, 1, 2, 1)[s] * (1 if way == CW else -1))
            inbox = rs_in.at[way, :, OWN, last]
            halved = pl.ds(way * half, half)
            if s == 2:
                own = last_piece(d).at[halved]
                own[...] = (own[...].astype(F32) + inbox[0, halved].astype(F32)).astype(BF16)
                own = last_piece(d)
                own[...] = (own[...].astype(F32) + inbox[1].astype(F32)).astype(BF16)
            rows = halved if s == 0 else pl.ds(0, width)
            send(last_piece(d).at[rows], inbox.at[s, rows], rs_sem.at[s, OWN, last], relay)

    def adam(c):
        if "state" not in waited:
            waited.add("state")
            loaded(NY + 2, state)
        columns = pl.ds(c * width, width)
        if c == last:
            zf_add(0)
        own = rs_sum(c, OWN)
        if c != last:
            wait(width, z_sem.at[c])
            own = own + z_in[c].astype(F32)
        gradient = own.T
        new_one = 0.9 * m_v[:, columns] + 0.1 * gradient
        new_two = 0.95 * s_v[:, columns] + 0.05 * gradient * gradient
        power = jnp.full(new_one.shape, step[0] + 1, jnp.int32).astype(F32)
        corr_one = 1.0 - jnp.exp(power * math.log(0.9))
        corr_two = 1.0 - jnp.exp(power * math.log(0.95))
        updated = w_v[:, columns] - 0.01 * (new_one / corr_one) / (jnp.sqrt(new_two / corr_two) + 1e-08)
        mate_send[c] = updated.astype(BF16)
        send(mate_send.at[c], mate_in.at[c], mate_sem.at[c], mate(mask))
        w_v[:, columns] = updated
        first_v[0, :, columns] = new_one
        second_v[0, :, columns] = new_two

    mine = lax.rem(r // mask, 2)

    def rows_of(d, c, zz, start, rows):
        return weights.at[d % NY, c // 2, pl.ds(zz * depth + start, rows), pl.ds((c % 2) * width, width)]

    def ring(d, c, zz):
        if c in shared:
            return rows_of(d, c, zz, pl.multiple_of(mine * (depth // 2), depth // 2), depth // 2)
        return rows_of(d, c, zz, 0, depth)

    def mix(c):
        columns = pl.ds(c * width, width)
        wait(depth, mate_sem.at[c])
        mixed = 0.5 * (w_v[:, columns] + mate_in[c].astype(F32))
        mixed_v[0, :, columns] = mixed
        rows_of(0, c, OWN, 0, depth)[...] = mixed.astype(BF16)
        send(ring(0, c, OWN), ring(0, c, OTHER), gz_sem.at[c], across)

    def once(key, rows, sem):
        if key not in waited:
            waited.add(key)
            wait(rows, sem)

    def ag_wait(d, c, zz):
        rows = depth // 2 if c in shared else depth
        if d != 0:
            once((abs(d), c, zz), rows if d == 4 else 2 * rows, ag_sem.at[abs(d) - 1, zz, c])
        elif zz == OTHER:
            once((0, c, zz), rows, gz_sem.at[c])

    def ag_send(have, there, way, c, zz):
        device = at_y(abs(have - there) * (1 if way == CW else -1))
        send(ring(have, c, zz), ring(there, c, zz), ag_sem.at[abs(there) - 1, zz, c], device)

    def ag(s, *pieces):
        for c, zz in pieces:
            for way in (CW, CCW):
                if s == 4 and zz == far_half(way):
                    continue
                have, there = (1 - s, -s) if way == CW else (s - 1, s)
                ag_wait(have, c, zz)
                ag_send(have, there, way, c, zz)

    def skip(stage, *pieces):
        for c, zz in pieces:
            for way in (CW, CCW):
                sign = -1 if way == CW else 1
                if stage == 1:
                    ag_wait(0, c, zz)
                    ag_send(0, 2 * sign, way, c, zz)
                else:
                    ag_wait(2 * sign, c, zz)
                    if zz != far_half(way):
                        ag_send(2 * sign, 4 * sign, way, c, zz)
            for way in (CW, CCW):
                sign = -1 if way == CW else 1
                if stage == 1:
                    ag_send(0, sign, way, c, zz)
                else:
                    ag_send(2 * sign, 3 * sign, way, c, zz)

    def fwd(c, d, zz):
        ag_wait(d, c, zz)
        there = ring(d, c, zz)
        send(there, there, fwd_sem.at[c // 2, abs(d)], mate(mask))

    def multiply(pair, *ds):
        for d in ds:
            for c in (2 * pair, 2 * pair + 1):
                for zz in (OWN, OTHER):
                    ag_wait(d, c, zz)
            passed = sum(c in shared for c in (2 * pair, 2 * pair + 1)) * (1, 4, 4, 4, 2)[abs(d)]
            if passed:
                once(("passed", pair, abs(d)), passed * (depth // 2), fwd_sem.at[pair, abs(d)])
            term = jnp.dot(x[d % NY], weights[d % NY, pair], preferred_element_type=F32)
            if d == 0:
                total[pair] = term
            elif d != 4:
                total[pair] += term
            else:
                keys[0, :, pl.ds(pair * 2 * width, 2 * width)] = (total[pair] + term).astype(BF16)

    w0, o0, w1, o1 = (0, OWN), (0, OTHER), (1, OWN), (1, OTHER)
    w2, o2, w3, o3 = (2, OWN), (2, OTHER), (3, OWN), (3, OTHER)

    prepare()
    if mask == 1:
        partial(4)
        enter()
        rs(0, o1)
        partial(0)
        rs(0, w1, o2, w0)
        zf_send(0)
        rs(0, w2, o0)
        partial(-2)
        partial(3)
        partial(-3)
        zf_send(3)
        partial(2)
        zf_send(2)
        partial(1)
        rs(1, o1)
        zf_send(4)
        partial(-1)
        rs(1, o2, w1)
        zf_send(-3)
        zf_send(1)
        rs(1, o0, w0)
        zf_send(-2)
        zf_send(-1)
        rs(1, w2)
        rs(2, o1, o2, w1, o0, w0, w2)
        rs(3, o1, o2)
        zf_rs(0)
        rs(3, w1, o0)
        zf_rs(1)
        rs(3, w0, w2)
        rs_across(1)
        rs_across(2)
        zf_rs(3)
        rs_across(0)
        zf_rs(2)
        adam(1)
        adam(2)
        adam(3)
        adam(0)
        mix(1)
        ag(1, w1)
        mix(2)
        ag(1, w2)
        mix(3)
        ag(1, w3)
        mix(0)
        ag(1, w0)
        fwd(1, 1, OWN)
        ag(2, w1)
        fwd(1, -1, OWN)
        ag(2, w2)
        fwd(2, 1, OWN)
        fwd(2, -1, OWN)
        ag(2, w3)
        fwd(3, -1, OWN)
        fwd(3, 1, OWN)
        ag(2, w0)
        fwd(0, -1, OWN)
        skip(1, o1)
        fwd(1, 0, OTHER)
        fwd(0, 1, OWN)
        ag(3, w1)
        fwd(1, 2, OWN)
        fwd(1, -2, OWN)
        skip(1, o2)
        fwd(2, 0, OTHER)
        ag(3, w2)
        fwd(2, -2, OWN)
        fwd(2, 2, OWN)
        skip(1, o3)
        fwd(3, 0, OTHER)
        ag(3, w3)
        fwd(3, 2, OWN)
        fwd(3, -2, OWN)
        fwd(0, 0, OTHER)
        skip(1, o0)
        ag(3, w0)
        fwd(0, 2, OWN)
        fwd(0, -2, OWN)
        fwd(1, -1, OTHER)
        fwd(1, 1, OTHER)
        fwd(1, -3, OWN)
        ag(4, w1)
        fwd(1, 3, OWN)
        fwd(1, 2, OTHER)
        skip(2, o1)
        fwd(1, -2, OTHER)
        multiply(1, 0)
        multiply(0, 0)
        fwd(2, 1, OTHER)
        fwd(2, -1, OTHER)
        ag(4, w2)
        fwd(2, -3, OWN)
        fwd(2, 3, OWN)
        fwd(2, -2, OTHER)
        fwd(2, 2, OTHER)
        skip(2, o2)
        fwd(3, -1, OTHER)
        fwd(3, 1, OTHER)
        ag(4, w3)
        fwd(3, 3, OWN)
        fwd(3, -3, OWN)
        skip(2, o3)
        fwd(3, -2, OTHER)
        fwd(3, 2, OTHER)
        fwd(0, 1, OTHER)
        fwd(0, -1, OTHER)
        ag(4, w0)
        fwd(0, 3, OWN)
        fwd(0, -3, OWN)
        skip(2, o0)
        fwd(1, 4, OWN)
        fwd(0, -2, OTHER)
        fwd(0, 2, OTHER)
        fwd(1, -3, OTHER)
        multiply(1, -1, 1)
        fwd(2, 4, OWN)
        fwd(1, 3, OTHER)
        fwd(2, -3, OTHER)
        multiply(1, -2, 2)
        fwd(3, 4, OWN)
        fwd(1, 4, OTHER)
        fwd(2, 3, OTHER)
        multiply(0, 1, -1)
        fwd(3, -3, OTHER)
        fwd(2, 4, OTHER)
        fwd(3, 3, OTHER)
        multiply(0, -2, 2)
        fwd(0, 4, OWN)
        fwd(0, -3, OTHER)
        fwd(3, 4, OTHER)
        fwd(0, 3, OTHER)
        fwd(0, 4, OTHER)
        multiply(1, -3, 3)
        multiply(0, -3)
        multiply(1, 4)
        multiply(0, 3, 4)
    else:
        partial(4)
        enter()
        rs(0, o1, w1, w0, o2, o0)
        partial(-3)
        rs(0, w2)
        partial(3)
        partial(-1)
        zf_send(3)
        partial(-2)
        partial(0)
        partial(2)
        rs(1, o1, w1)
        zf_send(2)
        zf_send(-1)
        zf_send(-2)
        zf_send(-3)
        rs(1, o2, w0)
        zf_send(0)
        zf_send(4)
        partial(1)
        rs(1, o0, w2)
        zf_send(1)
        rs(2, o1, w1, o2, w0, o0, w2)
        rs(3, o1, w1, o2, w0, o0, w2)
        zf_rs(1)
        rs_across(1)
        rs_across(2)
        zf_rs(0)
        rs_across(0)
        zf_rs(3)
        zf_rs(2)
        adam(1)
        adam(2)
        adam(0)
        mix(1)
        ag(1, w1)
        mix(2)
        ag(1, w2)
        adam(3)
        mix(0)
        ag(1, w0)
        fwd(1, -1, OWN)
        ag(2, w1)
        fwd(1, 1, OWN)
        ag(2, w2)
        fwd(2, 1, OWN)
        fwd(2, -1, OWN)
        mix(3)
        ag(1, w3)
        fwd(0, 1, OWN)
        ag(2, w0)
        fwd(0, -1, OWN)
        skip(1, o1)
        fwd(1, 0, OTHER)
        ag(3, w1)
        fwd(1, 2, OWN)
        fwd(1, -2, OWN)
        skip(1, o2)
        fwd(2, 0, OTHER)
        ag(3, w2)
        fwd(2, 2, OWN)
        fwd(2, -2, OWN)
        skip(1, o0)
        ag(2, w3)
        fwd(0, 0, OTHER)
        ag(3, w0)
        fwd(0, -2, OWN)
        fwd(0, 2, OWN)
        fwd(1, -1, OTHER)
        fwd(1, 1, OTHER)
        fwd(1, -3, OWN)
        fwd(1, 3, OWN)
        ag(4, w1)
        skip(2, o1)
        fwd(1, -2, OTHER)
        fwd(1, 2, OTHER)
        fwd(2, 1, OTHER)
        fwd(2, -1, OTHER)
        ag(4, w2)
        skip(1, o3)
        fwd(2, -3, OWN)
        fwd(2, 2, OTHER)
        multiply(0, 0)
        fwd(2, 3, OWN)
        fwd(2, -2, OTHER)
        multiply(1, 0)
        skip(2, o2)
        fwd(0, -1, OTHER)
        fwd(0, 1, OTHER)
        skip(2, o0)
        ag(3, w3)
        fwd(0, 2, OTHER)
        ag(4, w0)
        fwd(0, 3, OWN)
        fwd(0, -3, OWN)
        fwd(0, -2, OTHER)
        fwd(1, 4, OWN)
        fwd(1, -3, OTHER)
        fwd(1, 3, OTHER)
        fwd(2, 4, OWN)
        fwd(1, 4, OTHER)
        multiply(1, 1, -1)
        skip(2, o3)
        multiply(1, -2)
        fwd(2, -3, OTHER)
        fwd(0, -3, OTHER)
        multiply(1, 2)
        multiply(0, 2)
        fwd(2, 3, OTHER)
        multiply(0, -1, 1)
        ag(4, w3)
        fwd(2, 4, OTHER)
        fwd(0, 4, OWN)
        multiply(0, -2)
        fwd(0, 3, OTHER)
        fwd(0, 4, OTHER)
        multiply(1, -3)
        multiply(0, -3)
        multiply(1, 3, 4)
        multiply(0, 3, 4)

    wait(sum(sent), send_sem.at[0])


def store(*refs):
    count = len(refs) // 2
    sem = refs[-1]
    copies = [pltpu.make_async_copy(refs[i], refs[count + i], sem.at[i]) for i in range(count)]
    for copy in copies:
        copy.start()
    for copy in copies:
        copy.wait()


def on_device(inputs, key_grads, token_ids, step, master, first_moment, second_moment):
    tokens, features = inputs.shape[1:]
    depth, columns = master.shape[1:]
    width = columns // NC
    hbm = pl.BlockSpec(memory_space=pltpu.HBM)
    vmem = pl.BlockSpec(memory_space=pltpu.VMEM)
    any_space = pl.BlockSpec(memory_space=pl.ANY)
    dma = pltpu.SemaphoreType.DMA
    shapes = [(master.shape, F32)] * 3 + [((1, tokens, columns), BF16)]

    def with_partner(bit, *operands):
        mask = PARTNERS[bit]
        shared = SHARED[bit]
        results = pl.pallas_call(
            functools.partial(kernel, mask, shared),
            out_shape=[pltpu.VMEM(shape, dtype) for shape, dtype in shapes],
            in_specs=[hbm] * 3 + [pl.BlockSpec(memory_space=pltpu.SMEM)] + [hbm] * 3,
            out_specs=[vmem] * 4,
            scratch_shapes=[
                pltpu.VMEM((NY, tokens, 2 * depth), BF16),
                pltpu.VMEM((tokens, columns), BF16),
                pltpu.VMEM((1, tokens), jnp.int32),
                pltpu.VMEM((columns, tokens), BF16),
                pltpu.VMEM((NY, 2, columns, depth), BF16),
                pltpu.VMEM((2, 4, 2, NC, width, depth), BF16),
                pltpu.VMEM((NY, width, depth), BF16),
                pltpu.VMEM((NY, NC // 2, 2 * depth, 2 * width), BF16),
                pltpu.VMEM((NC // 2, tokens, 2 * width), F32),
                pltpu.VMEM((NC, width, depth), BF16),
                pltpu.VMEM((NC, width, depth), BF16),
                pltpu.VMEM((NC, depth, width), BF16),
                pltpu.VMEM((NC, depth, width), BF16),
                pltpu.VMEM((3, depth, columns), F32),
                pltpu.VMEM((NC * 32 * depth, depth), BF16),
                dma((NY + 3,)),
                dma((1,)),
                dma((4, 2, NC)),
                dma((4, 2, NC)),
                dma((NC,)),
                dma((NC,)),
                dma((NC,)),
                dma((5,)),
                dma((NC // 2, 5)),
            ],
            compiler_params=pltpu.CompilerParams(
                collective_id=bit, has_side_effects=True, vmem_limit_bytes=58 * 2**20
            ),
            cost_estimate=pl.CostEstimate(
                flops=4 * tokens * features * columns, bytes_accessed=5 * 2**20, transcendentals=0
            ),
            name="grad_adam_keys",
        )(*operands)
        results = [pltpu.with_memory_space_constraint(result, pltpu.VMEM) for result in results]
        return pl.pallas_call(
            store,
            out_shape=[jax.ShapeDtypeStruct(shape, dtype) for shape, dtype in shapes],
            in_specs=[any_space] * 4,
            out_specs=[any_space] * 4,
            scratch_shapes=[dma((4,))],
            name="store_results",
        )(*results)

    branches = [functools.partial(with_partner, bit) for bit in range(len(PARTNERS))]
    return lax.switch(
        lax.rem(step, len(PARTNERS)), branches,
        inputs, key_grads, token_ids, step.reshape(1), master, first_moment, second_moment,
    )


def solution(mesh):
    in_specs = (
        P("rep", "fsdp", None),
        P("rep", "fsdp", None),
        P("rep", "fsdp"),
        P(),
        P("rep", "fsdp", None),
        P("rep", "fsdp", None),
        P("rep", "fsdp", None),
    )
    out_specs = (
        P("rep", "fsdp", None),
        P("rep", "fsdp", None),
        P("rep", "fsdp", None),
        P("rep", "fsdp", None),
    )
    return jax.shard_map(
        on_device, mesh=mesh, in_specs=in_specs, out_specs=out_specs, check_vma=False
    )
```

```python
import functools
import functools
import math

import jax
import jax.numpy as jnp
from jax import lax
from jax.experimental import pallas as pl
from jax.experimental.pallas import tpu as pltpu
from jax.sharding import PartitionSpec as P

MESH = pl.DeviceIdType.MESH
F32, BF16 = jnp.float32, jnp.bfloat16

NY = 8
NC = 4
OWN, OTHER = 0, 1
CW, CCW = 0, 1
PARTNERS = (1, 2, 4, 8)
SHARED = ((0, 1, 2, 3), (0, 1, 2), (0, 1, 2), (0, 1, 2))


def kernel(
    mask, shared, inputs, grads, ids, step, master, first, second,
    mixed_v, first_v, second_v, keys,
    x, g, idv, gt, part, rs_in, zf_in, weights, total, z_send, z_in, mate_send, mate_in, state, count,
    load_sem, send_sem, rs_sem, ag_sem, z_sem, mate_sem, gz_sem, zf_sem, fwd_sem,
):
    w_v, m_v, s_v = state.at[0], state.at[1], state.at[2]
    depth = w_v.shape[0]
    width = w_v.shape[1] // NC
    r, f = lax.axis_index("rep"), lax.axis_index("fsdp")
    y, z = lax.rem(f, NY), f // NY

    def at_y(d):
        return (r, z * NY + lax.rem(y + d + NY, NY))

    across = (r, (1 - z) * NY + y)

    def mate(mask):
        return (r + mask - 2 * mask * lax.rem(r // mask, 2), f)

    towards = (at_y(1), at_y(-1))

    def load(i, source, target):
        pltpu.make_async_copy(source, target, load_sem.at[i]).start()

    def loaded(i, target):
        pltpu.make_async_copy(target, target, load_sem.at[i]).wait()

    def load_inputs(*ds):
        for d in ds:
            for zz in (OWN, OTHER):
                plane = z if zz == OWN else 1 - z
                column = pl.multiple_of((plane * NY + lax.rem(y + d + NY, NY)) * depth, depth)
                load(d % NY, inputs.at[0, :, pl.ds(column, depth)], x.at[d % NY, :, pl.ds(zz * depth, depth)])

    load(NY, grads.at[0], g)
    load(NY + 1, ids, idv)
    load_inputs(4)
    barrier = pltpu.get_barrier_semaphore()
    peers = [*towards, at_y(2), at_y(-2), across, mate(mask)]
    for peer in peers:
        pl.semaphore_signal(barrier, inc=1, device_id=peer, device_id_type=MESH)
    load_inputs(3, -3, 2, -2, 1, -1, 0)
    load(NY + 2, master.at[0], w_v)
    load(NY + 2, first.at[0], m_v)
    load(NY + 2, second.at[0], s_v)

    sent = []
    waited = set()

    def send(source, target, sem, device):
        copy = pltpu.make_async_remote_copy(source, target, send_sem.at[0], sem, device_id=device, device_id_type=MESH)
        copy.start()
        sent.append(math.prod(source.shape) // depth)

    def wait(rows, sem):
        some = count.at[pl.ds(0, rows)]
        pltpu.make_async_copy(some, some, sem).wait()

    def prepare():
        loaded(NY, g)
        loaded(NY + 1, idv)
        live = (idv[...] != 0).astype(F32)
        gt[...] = (g[...].astype(F32).T * live).astype(BF16)

    def partial(d):
        loaded(d % NY, x.at[d % NY])
        product = jnp.dot(gt[...], x[d % NY], preferred_element_type=F32).astype(BF16)
        part[d % NY, OWN] = product[:, :depth]
        part[d % NY, OTHER] = product[:, depth:]

    def enter():
        pl.semaphore_wait(barrier, len(peers))

    def far_half(way):
        return OTHER if way == CW else OWN

    def rs(s, *pieces):
        for c, zz in pieces:
            if s > 0:
                wait(width if s == 1 else 2 * width, rs_sem.at[s - 1, zz, c])
            for way in (CW, CCW):
                if s == 0 and zz != far_half(way):
                    continue
                d = (4 - s) if way == CW else (s - 4)
                own = part.at[d % NY, zz, pl.ds(c * width, width)]
                if s > 1 or (s == 1 and zz == far_half(way)):
                    own[...] = (own[...].astype(F32) + rs_in[way, s - 1, zz, c].astype(F32)).astype(BF16)
                send(own, rs_in.at[way, s, zz, c], rs_sem.at[s, zz, c], towards[way])

    relayed = {(NC - 1, OWN)}

    def rskip(s, *pieces):
        for c, zz in pieces:
            relayed.add((c, zz))
            if s == 2:
                wait(width, rs_sem.at[0, zz, c])
                wait(2 * width, rs_sem.at[1, zz, c])
            for way in (CW, CCW):
                if s == 0 and zz != far_half(way):
                    continue
                d = (4 - s) if way == CW else (s - 4)
                own = part.at[d % NY, zz, pl.ds(c * width, width)]
                if s == 2:
                    value = own[...].astype(F32) + rs_in[way, 1, zz, c].astype(F32)
                    if zz == far_half(way):
                        value = value + rs_in[way, 0, zz, c].astype(F32)
                    own[...] = value.astype(BF16)
                relay = at_y((2, 1, 2, 1)[s] * (1 if way == CW else -1))
                send(own, rs_in.at[way, s, zz, c], rs_sem.at[s, zz, c], relay)

    def rs_sum(c, zz):
        own = part[0, zz, pl.ds(c * width, width)].astype(F32)
        for s in (2, 3) if (c, zz) in relayed else (3,):
            wait(2 * width, rs_sem.at[s, zz, c])
            for way in (CW, CCW):
                own = own + rs_in[way, s, zz, c].astype(F32)
        return own

    def rs_across(c):
        z_send[c] = rs_sum(c, OTHER).astype(BF16)
        send(z_send.at[c], z_in.at[c], z_sem.at[c], across)

    last = NC - 1
    half = width // 2

    def last_piece(d):
        return part.at[d % NY, OWN, pl.ds(last * width, width)]

    def zf_send(d):
        send(part.at[d % NY, OTHER, pl.ds(last * width, width)], zf_in.at[d % NY], zf_sem.at[abs(d)], across)

    def zf_add(*ds):
        wait(len(ds) * width, zf_sem.at[abs(ds[0])])
        for d in ds:
            own = last_piece(d)
            own[...] = (own[...].astype(F32) + zf_in[d % NY].astype(F32)).astype(BF16)

    def zf_rs(s):
        zf_add(*((4,) if s == 0 else (4 - s, s - 4)))
        if s == 2:
            wait(width, rs_sem.at[0, OWN, last])
            wait(2 * width, rs_sem.at[1, OWN, last])
        for way in (CW, CCW):
            d = (4 - s) if way == CW else (s - 4)
            relay = at_y((2, 1, 2, 1)[s] * (1 if way == CW else -1))
            inbox = rs_in.at[way, :, OWN, last]
            halved = pl.ds(way * half, half)
            if s == 2:
                own = last_piece(d).at[halved]
                own[...] = (own[...].astype(F32) + inbox[0, halved].astype(F32)).astype(BF16)
                own = last_piece(d)
                own[...] = (own[...].astype(F32) + inbox[1].astype(F32)).astype(BF16)
            rows = halved if s == 0 else pl.ds(0, width)
            send(last_piece(d).at[rows], inbox.at[s, rows], rs_sem.at[s, OWN, last], relay)

    def adam(c):
        if "state" not in waited:
            waited.add("state")
            loaded(NY + 2, state)
        columns = pl.ds(c * width, width)
        if c == last:
            zf_add(0)
        own = rs_sum(c, OWN)
        if c != last:
            wait(width, z_sem.at[c])
            own = own + z_in[c].astype(F32)
        gradient = own.T
        new_one = 0.9 * m_v[:, columns] + 0.1 * gradient
        new_two = 0.95 * s_v[:, columns] + 0.05 * gradient * gradient
        power = jnp.full(new_one.shape, step[0] + 1, jnp.int32).astype(F32)
        corr_one = 1.0 - jnp.exp(power * math.log(0.9))
        corr_two = 1.0 - jnp.exp(power * math.log(0.95))
        updated = w_v[:, columns] - 0.01 * (new_one / corr_one) / (jnp.sqrt(new_two / corr_two) + 1e-08)
        mate_send[c] = updated.astype(BF16)
        send(mate_send.at[c], mate_in.at[c], mate_sem.at[c], mate(mask))
        w_v[:, columns] = updated
        first_v[0, :, columns] = new_one
        second_v[0, :, columns] = new_two

    mine = lax.rem(r // mask, 2)

    def rows_of(d, c, zz, start, rows):
        return weights.at[d % NY, c // 2, pl.ds(zz * depth + start, rows), pl.ds((c % 2) * width, width)]

    def ring(d, c, zz):
        if c in shared:
            return rows_of(d, c, zz, pl.multiple_of(mine * (depth // 2), depth // 2), depth // 2)
        return rows_of(d, c, zz, 0, depth)

    def mix(c):
        columns = pl.ds(c * width, width)
        wait(depth, mate_sem.at[c])
        mixed = 0.5 * (w_v[:, columns] + mate_in[c].astype(F32))
        mixed_v[0, :, columns] = mixed
        rows_of(0, c, OWN, 0, depth)[...] = mixed.astype(BF16)
        send(ring(0, c, OWN), ring(0, c, OTHER), gz_sem.at[c], across)

    def once(key, rows, sem):
        if key not in waited:
            waited.add(key)
            wait(rows, sem)

    def ag_wait(d, c, zz):
        rows = depth // 2 if c in shared else depth
        if d != 0:
            once((abs(d), c, zz), rows if d == 4 else 2 * rows, ag_sem.at[abs(d) - 1, zz, c])
        elif zz == OTHER:
            once((0, c, zz), rows, gz_sem.at[c])

    def ag_send(have, there, way, c, zz):
        device = at_y(abs(have - there) * (1 if way == CW else -1))
        send(ring(have, c, zz), ring(there, c, zz), ag_sem.at[abs(there) - 1, zz, c], device)

    def ag(s, *pieces):
        for c, zz in pieces:
            for way in (CW, CCW):
                if s == 4 and zz == far_half(way):
                    continue
                have, there = (1 - s, -s) if way == CW else (s - 1, s)
                ag_wait(have, c, zz)
                ag_send(have, there, way, c, zz)

    def skip(stage, *pieces):
        for c, zz in pieces:
            for way in (CW, CCW):
                sign = -1 if way == CW else 1
                if stage == 1:
                    ag_wait(0, c, zz)
                    ag_send(0, 2 * sign, way, c, zz)
                else:
                    ag_wait(2 * sign, c, zz)
                    if zz != far_half(way):
                        ag_send(2 * sign, 4 * sign, way, c, zz)
            for way in (CW, CCW):
                sign = -1 if way == CW else 1
                if stage == 1:
                    ag_send(0, sign, way, c, zz)
                else:
                    ag_send(2 * sign, 3 * sign, way, c, zz)

    def fwd(c, d, zz):
        ag_wait(d, c, zz)
        there = ring(d, c, zz)
        send(there, there, fwd_sem.at[c // 2, abs(d)], mate(mask))

    def multiply(pair, *ds):
        for d in ds:
            for c in (2 * pair, 2 * pair + 1):
                for zz in (OWN, OTHER):
                    ag_wait(d, c, zz)
            passed = sum(c in shared for c in (2 * pair, 2 * pair + 1)) * (1, 4, 4, 4, 2)[abs(d)]
            if passed:
                once(("passed", pair, abs(d)), passed * (depth // 2), fwd_sem.at[pair, abs(d)])
            term = jnp.dot(x[d % NY], weights[d % NY, pair], preferred_element_type=F32)
            if d == 0:
                total[pair] = term
            elif d != 4:
                total[pair] += term
            else:
                keys[0, :, pl.ds(pair * 2 * width, 2 * width)] = (total[pair] + term).astype(BF16)

    w0, o0, w1, o1 = (0, OWN), (0, OTHER), (1, OWN), (1, OTHER)
    w2, o2, w3, o3 = (2, OWN), (2, OTHER), (3, OWN), (3, OTHER)

    prepare()
    if mask == 1:
        partial(4)
        enter()
        rs(0, o0, o1, o2)
        partial(-3)
        rs(0, w0, w2)
        partial(2)
        rs(0, w1)
        partial(3)
        zf_send(4)
        zf_send(-3)
        partial(-2)
        zf_send(3)
        partial(0)
        zf_send(-2)
        partial(1)
        rs(1, o0)
        partial(-1)
        rs(1, o1, w0)
        zf_send(2)
        zf_send(-1)
        zf_send(0)
        rs(1, o2, w2)
        zf_send(1)
        rs(1, w1)
        rs(2, o0, o1, w0)
        zf_rs(0)
        rs(2, o2, w2, w1)
        rs(3, o0)
        zf_rs(1)
        rs(3, o1, w0, o2, w2, w1)
        rs_across(0)
        zf_rs(2)
        rs_across(1)
        zf_rs(3)
        rs_across(2)
        adam(3)
        adam(0)
        mix(3)
        skip(1, w3)
        adam(1)
        mix(0)
        ag(1, w0)
        adam(2)
        mix(1)
        ag(1, w1)
        mix(2)
        skip(1, w2)
        fwd(3, -1, OWN)
        fwd(3, 1, OWN)
        ag(2, w0)
        skip(2, w3)
        fwd(3, 2, OWN)
        fwd(3, -2, OWN)
        fwd(0, -1, OWN)
        fwd(0, 1, OWN)
        fwd(1, -1, OWN)
        ag(2, w1)
        fwd(1, 1, OWN)
        skip(1, o3)
        fwd(3, 0, OTHER)
        skip(1, o0)
        fwd(0, 0, OTHER)
        fwd(2, -1, OWN)
        fwd(2, 1, OWN)
        ag(3, w0)
        fwd(0, -2, OWN)
        fwd(3, 3, OWN)
        fwd(1, 0, OTHER)
        skip(1, o1)
        fwd(1, 2, OWN)
        fwd(3, -3, OWN)
        fwd(2, 2, OWN)
        fwd(0, 2, OWN)
        fwd(1, -2, OWN)
        fwd(3, 4, OWN)
        multiply(0, 0)
        skip(1, o2)
        fwd(2, 0, OTHER)
        ag(3, w1)
        fwd(3, 1, OTHER)
        fwd(3, -1, OTHER)
        fwd(2, -2, OWN)
        skip(2, w2)
        fwd(3, 2, OTHER)
        multiply(1, 0)
        skip(2, o3)
        fwd(3, -2, OTHER)
        fwd(0, 1, OTHER)
        fwd(0, -3, OWN)
        skip(2, o0)
        fwd(0, 2, OTHER)
        fwd(0, 3, OWN)
        ag(4, w0)
        fwd(0, -2, OTHER)
        fwd(0, -1, OTHER)
        fwd(1, 1, OTHER)
        fwd(1, -1, OTHER)
        fwd(1, 2, OTHER)
        fwd(1, -2, OTHER)
        skip(2, o1)
        multiply(0, -1)
        fwd(2, 1, OTHER)
        multiply(0, 1, 2)
        fwd(2, -2, OTHER)
        fwd(1, -3, OWN)
        fwd(1, 3, OWN)
        skip(2, o2)
        multiply(0, -2)
        fwd(2, 2, OTHER)
        ag(4, w1)
        fwd(2, -3, OWN)
        fwd(2, -1, OTHER)
        fwd(2, 3, OWN)
        fwd(3, -3, OTHER)
        fwd(3, 3, OTHER)
        fwd(2, 4, OWN)
        fwd(0, -3, OTHER)
        multiply(1, 2, -1, 1)
        fwd(1, -3, OTHER)
        multiply(1, -2)
        fwd(0, 4, OWN)
        fwd(3, 4, OTHER)
        fwd(0, 3, OTHER)
        fwd(0, 4, OTHER)
        fwd(1, 3, OTHER)
        fwd(2, -3, OTHER)
        fwd(1, 4, OTHER)
        fwd(1, 4, OWN)
        multiply(0, -3)
        fwd(2, 3, OTHER)
        multiply(0, 3)
        fwd(2, 4, OTHER)
        multiply(0, 4)
        multiply(1, 3, -3, 4)
    elif mask in (2, 4):
        partial(4)
        enter()
        rs(0, o1, w1, w0, o2, o0)
        partial(-3)
        rs(0, w2)
        partial(3)
        partial(-1)
        zf_send(3)
        partial(-2)
        partial(0)
        partial(2)
        rs(1, o1, w1)
        zf_send(2)
        zf_send(-1)
        zf_send(-2)
        zf_send(-3)
        rs(1, o2, w0)
        zf_send(0)
        zf_send(4)
        partial(1)
        rs(1, o0, w2)
        zf_send(1)
        rs(2, o1, w1, o2, w0, o0, w2)
        rs(3, o1, w1, o2, w0, o0, w2)
        zf_rs(1)
        rs_across(1)
        rs_across(2)
        zf_rs(0)
        rs_across(0)
        zf_rs(3)
        zf_rs(2)
        adam(1)
        adam(2)
        adam(0)
        mix(1)
        ag(1, w1)
        mix(2)
        ag(1, w2)
        adam(3)
        mix(0)
        ag(1, w0)
        fwd(1, -1, OWN)
        ag(2, w1)
        fwd(1, 1, OWN)
        ag(2, w2)
        fwd(2, 1, OWN)
        fwd(2, -1, OWN)
        mix(3)
        ag(1, w3)
        fwd(0, 1, OWN)
        ag(2, w0)
        fwd(0, -1, OWN)
        skip(1, o1)
        fwd(1, 0, OTHER)
        ag(3, w1)
        fwd(1, 2, OWN)
        fwd(1, -2, OWN)
        skip(1, o2)
        fwd(2, 0, OTHER)
        ag(3, w2)
        fwd(2, 2, OWN)
        fwd(2, -2, OWN)
        skip(1, o0)
        ag(2, w3)
        fwd(0, 0, OTHER)
        ag(3, w0)
        fwd(0, -2, OWN)
        fwd(0, 2, OWN)
        fwd(1, -1, OTHER)
        fwd(1, 1, OTHER)
        fwd(1, -3, OWN)
        fwd(1, 3, OWN)
        ag(4, w1)
        skip(2, o1)
        fwd(1, -2, OTHER)
        fwd(1, 2, OTHER)
        fwd(2, 1, OTHER)
        fwd(2, -1, OTHER)
        ag(4, w2)
        skip(1, o3)
        fwd(2, -3, OWN)
        fwd(2, 2, OTHER)
        multiply(0, 0)
        fwd(2, 3, OWN)
        fwd(2, -2, OTHER)
        multiply(1, 0)
        skip(2, o2)
        fwd(0, -1, OTHER)
        fwd(0, 1, OTHER)
        skip(2, o0)
        ag(3, w3)
        fwd(0, 2, OTHER)
        ag(4, w0)
        fwd(0, 3, OWN)
        fwd(0, -3, OWN)
        fwd(0, -2, OTHER)
        fwd(1, 4, OWN)
        fwd(1, -3, OTHER)
        fwd(1, 3, OTHER)
        fwd(2, 4, OWN)
        fwd(1, 4, OTHER)
        multiply(1, 1, -1)
        skip(2, o3)
        multiply(1, -2)
        fwd(2, -3, OTHER)
        fwd(0, -3, OTHER)
        multiply(1, 2)
        multiply(0, 2)
        fwd(2, 3, OTHER)
        multiply(0, -1, 1)
        ag(4, w3)
        fwd(2, 4, OTHER)
        fwd(0, 4, OWN)
        multiply(0, -2)
        fwd(0, 3, OTHER)
        fwd(0, 4, OTHER)
        multiply(1, -3)
        multiply(0, -3)
        multiply(1, 3, 4)
        multiply(0, 3, 4)
    else:
        partial(4)
        enter()
        rs(0, o2, o0)
        partial(0)
        rs(0, w1)
        partial(-1)
        zf_send(-1)
        partial(-2)
        zf_send(-2)
        rs(0, o1)
        zf_send(0)
        partial(2)
        zf_send(2)
        rs(0, w0)
        partial(-3)
        zf_send(-3)
        partial(3)
        zf_send(3)
        rs(1, o2)
        rs(0, w2)
        zf_send(4)
        partial(1)
        rs(1, o0)
        zf_send(1)
        rs(1, w1, o1, w0)
        rs(2, o2)
        rs(1, w2)
        rs(2, o0, w1, o1, w0)
        rs(3, o2)
        rs(2, w2)
        rs(3, o0, w1, o1, w0)
        zf_rs(1)
        rs_across(2)
        rs(3, w2)
        zf_rs(0)
        rs_across(0)
        zf_rs(3)
        rs_across(1)
        zf_rs(2)
        adam(2)
        adam(0)
        adam(1)
        mix(2)
        ag(1, w2)
        adam(3)
        mix(0)
        ag(1, w0)
        mix(1)
        ag(1, w1)
        ag(2, w2)
        fwd(2, -1, OWN)
        fwd(2, 1, OWN)
        mix(3)
        ag(1, w3)
        ag(2, w0)
        fwd(0, -1, OWN)
        fwd(0, 1, OWN)
        ag(2, w1)
        fwd(1, 1, OWN)
        fwd(1, -1, OWN)
        skip(1, o2)
        ag(3, w2)
        fwd(2, 0, OTHER)
        fwd(2, -2, OWN)
        fwd(2, 2, OWN)
        skip(1, o0)
        fwd(0, 0, OTHER)
        ag(2, w3)
        ag(3, w0)
        fwd(0, -2, OWN)
        fwd(0, 2, OWN)
        skip(1, o1)
        ag(3, w1)
        fwd(1, -2, OWN)
        fwd(1, 0, OTHER)
        fwd(1, 2, OWN)
        fwd(2, 1, OTHER)
        fwd(2, -1, OTHER)
        ag(4, w2)
        fwd(2, 3, OWN)
        fwd(2, -3, OWN)
        skip(2, o2)
        fwd(2, 2, OTHER)
        fwd(2, -2, OTHER)
        skip(1, o3)
        multiply(1, 0)
        fwd(0, 1, OTHER)
        fwd(0, -1, OTHER)
        skip(2, o0)
        fwd(0, 2, OTHER)
        ag(3, w3)
        fwd(0, -2, OTHER)
        ag(4, w0)
        fwd(0, -3, OWN)
        multiply(0, 0)
        fwd(0, 3, OWN)
        fwd(1, -1, OTHER)
        fwd(1, 1, OTHER)
        ag(4, w1)
        fwd(1, -3, OWN)
        fwd(1, 3, OWN)
        fwd(1, 2, OTHER)
        skip(2, o1)
        fwd(1, -2, OTHER)
        fwd(2, 4, OWN)
        fwd(2, -3, OTHER)
        fwd(2, 3, OTHER)
        fwd(2, 4, OTHER)
        multiply(1, -1)
        fwd(0, -3, OTHER)
        skip(2, o3)
        multiply(1, 2, 1)
        ag(4, w3)
        multiply(0, -1, 1)
        fwd(0, 4, OWN)
        multiply(1, -2)
        fwd(0, 3, OTHER)
        fwd(1, 4, OWN)
        fwd(0, 4, OTHER)
        fwd(1, -3, OTHER)
        multiply(0, -2, 2)
        fwd(1, 3, OTHER)
        fwd(1, 4, OTHER)
        multiply(1, -3, 3, 4)
        multiply(0, 3, -3, 4)

    wait(sum(sent), send_sem.at[0])


def store(*refs):
    count = len(refs) // 2
    sem = refs[-1]
    copies = [pltpu.make_async_copy(refs[i], refs[count + i], sem.at[i]) for i in range(count)]
    for copy in copies:
        copy.start()
    for copy in copies:
        copy.wait()


def on_device(inputs, key_grads, token_ids, step, master, first_moment, second_moment):
    tokens, features = inputs.shape[1:]
    depth, columns = master.shape[1:]
    width = columns // NC
    hbm = pl.BlockSpec(memory_space=pltpu.HBM)
    vmem = pl.BlockSpec(memory_space=pltpu.VMEM)
    any_space = pl.BlockSpec(memory_space=pl.ANY)
    dma = pltpu.SemaphoreType.DMA
    shapes = [(master.shape, F32)] * 3 + [((1, tokens, columns), BF16)]

    def with_partner(bit, *operands):
        mask = PARTNERS[bit]
        shared = SHARED[bit]
        results = pl.pallas_call(
            functools.partial(kernel, mask, shared),
            out_shape=[pltpu.VMEM(shape, dtype) for shape, dtype in shapes],
            in_specs=[hbm] * 3 + [pl.BlockSpec(memory_space=pltpu.SMEM)] + [hbm] * 3,
            out_specs=[vmem] * 4,
            scratch_shapes=[
                pltpu.VMEM((NY, tokens, 2 * depth), BF16),
                pltpu.VMEM((tokens, columns), BF16),
                pltpu.VMEM((1, tokens), jnp.int32),
                pltpu.VMEM((columns, tokens), BF16),
                pltpu.VMEM((NY, 2, columns, depth), BF16),
                pltpu.VMEM((2, 4, 2, NC, width, depth), BF16),
                pltpu.VMEM((NY, width, depth), BF16),
                pltpu.VMEM((NY, NC // 2, 2 * depth, 2 * width), BF16),
                pltpu.VMEM((NC // 2, tokens, 2 * width), F32),
                pltpu.VMEM((NC, width, depth), BF16),
                pltpu.VMEM((NC, width, depth), BF16),
                pltpu.VMEM((NC, depth, width), BF16),
                pltpu.VMEM((NC, depth, width), BF16),
                pltpu.VMEM((3, depth, columns), F32),
                pltpu.VMEM((NC * 32 * depth, depth), BF16),
                dma((NY + 3,)),
                dma((1,)),
                dma((4, 2, NC)),
                dma((4, 2, NC)),
                dma((NC,)),
                dma((NC,)),
                dma((NC,)),
                dma((5,)),
                dma((NC // 2, 5)),
            ],
            compiler_params=pltpu.CompilerParams(
                collective_id=bit, has_side_effects=True, vmem_limit_bytes=58 * 2**20
            ),
            cost_estimate=pl.CostEstimate(
                flops=4 * tokens * features * columns, bytes_accessed=5 * 2**20, transcendentals=0
            ),
            name="grad_adam_keys",
        )(*operands)
        results = [pltpu.with_memory_space_constraint(result, pltpu.VMEM) for result in results]
        return pl.pallas_call(
            store,
            out_shape=[jax.ShapeDtypeStruct(shape, dtype) for shape, dtype in shapes],
            in_specs=[any_space] * 4,
            out_specs=[any_space] * 4,
            scratch_shapes=[dma((4,))],
            name="store_results",
        )(*results)

    branches = [functools.partial(with_partner, bit) for bit in range(len(PARTNERS))]
    return lax.switch(
        lax.rem(step, len(PARTNERS)), branches,
        inputs, key_grads, token_ids, step.reshape(1), master, first_moment, second_moment,
    )


def solution(mesh):
    in_specs = (
        P("rep", "fsdp", None),
        P("rep", "fsdp", None),
        P("rep", "fsdp"),
        P(),
        P("rep", "fsdp", None),
        P("rep", "fsdp", None),
        P("rep", "fsdp", None),
    )
    out_specs = (
        P("rep", "fsdp", None),
        P("rep", "fsdp", None),
        P("rep", "fsdp", None),
        P("rep", "fsdp", None),
    )
    return jax.shard_map(
        on_device, mesh=mesh, in_specs=in_specs, out_specs=out_specs, check_vma=False
    )
```

```python
import functools
import functools
import math

import jax
import jax.numpy as jnp
from jax import lax
from jax.experimental import pallas as pl
from jax.experimental.pallas import tpu as pltpu
from jax.sharding import PartitionSpec as P

MESH = pl.DeviceIdType.MESH
F32, BF16 = jnp.float32, jnp.bfloat16

NY = 8
NC = 4
OWN, OTHER = 0, 1
CW, CCW = 0, 1
PARTNERS = (1, 2, 4, 8)
SHARED = ((0, 1, 2, 3), (0, 1, 2), (0, 1, 2), (0, 1, 2))


def kernel(
    mask, shared, inputs, grads, ids, step, master, first, second,
    mixed_v, first_v, second_v, keys,
    x, g, idv, gt, part, rs_in, zf_in, weights, total, z_send, z_in, mate_send, mate_in, state, count,
    load_sem, send_sem, rs_sem, ag_sem, z_sem, mate_sem, gz_sem, zf_sem, fwd_sem,
):
    w_v, m_v, s_v = state.at[0], state.at[1], state.at[2]
    depth = w_v.shape[0]
    width = w_v.shape[1] // NC
    r, f = lax.axis_index("rep"), lax.axis_index("fsdp")
    y, z = lax.rem(f, NY), f // NY

    def at_y(d):
        return (r, z * NY + lax.rem(y + d + NY, NY))

    across = (r, (1 - z) * NY + y)

    def mate(mask):
        return (r + mask - 2 * mask * lax.rem(r // mask, 2), f)

    towards = (at_y(1), at_y(-1))

    def load(i, source, target):
        pltpu.make_async_copy(source, target, load_sem.at[i]).start()

    def loaded(i, target):
        pltpu.make_async_copy(target, target, load_sem.at[i]).wait()

    def load_inputs(*ds):
        for d in ds:
            for zz in (OWN, OTHER):
                plane = z if zz == OWN else 1 - z
                column = pl.multiple_of((plane * NY + lax.rem(y + d + NY, NY)) * depth, depth)
                load(d % NY, inputs.at[0, :, pl.ds(column, depth)], x.at[d % NY, :, pl.ds(zz * depth, depth)])

    barrier = pltpu.get_barrier_semaphore()
    peers = [across, mate(mask), at_y(2), at_y(-2), *towards]
    for peer in peers:
        pl.semaphore_signal(barrier, inc=1, device_id=peer, device_id_type=MESH)
    load(NY, grads.at[0], g)
    load(NY + 1, ids, idv)
    load_inputs(4)
    load_inputs(3, -3, 2, -2, 1, -1, 0)
    load(NY + 2, master.at[0], w_v)
    load(NY + 2, first.at[0], m_v)
    load(NY + 2, second.at[0], s_v)

    sent = []
    waited = set()

    def send(source, target, sem, device):
        copy = pltpu.make_async_remote_copy(source, target, send_sem.at[0], sem, device_id=device, device_id_type=MESH)
        copy.start()
        sent.append(math.prod(source.shape) // depth)

    def wait(rows, sem):
        some = count.at[pl.ds(0, rows)]
        pltpu.make_async_copy(some, some, sem).wait()

    def prepare():
        loaded(NY, g)
        loaded(NY + 1, idv)
        live = (idv[...] != 0).astype(F32)
        gt[...] = (g[...].astype(F32).T * live).astype(BF16)

    def partial(d):
        loaded(d % NY, x.at[d % NY])
        product = jnp.dot(gt[...], x[d % NY], preferred_element_type=F32).astype(BF16)
        part[d % NY, OWN] = product[:, :depth]
        part[d % NY, OTHER] = product[:, depth:]

    def enter():
        pl.semaphore_wait(barrier, len(peers))

    def far_half(way):
        return OTHER if way == CW else OWN

    def rs(s, *pieces):
        for c, zz in pieces:
            if s > 0:
                wait(width if s == 1 else 2 * width, rs_sem.at[s - 1, zz, c])
            for way in (CW, CCW):
                if s == 0 and zz != far_half(way):
                    continue
                d = (4 - s) if way == CW else (s - 4)
                own = part.at[d % NY, zz, pl.ds(c * width, width)]
                if s > 1 or (s == 1 and zz == far_half(way)):
                    own[...] = (own[...].astype(F32) + rs_in[way, s - 1, zz, c].astype(F32)).astype(BF16)
                send(own, rs_in.at[way, s, zz, c], rs_sem.at[s, zz, c], towards[way])

    relayed = {(NC - 1, OWN)}

    def rskip(s, *pieces):
        for c, zz in pieces:
            relayed.add((c, zz))
            if s == 2:
                wait(width, rs_sem.at[0, zz, c])
                wait(2 * width, rs_sem.at[1, zz, c])
            for way in (CW, CCW):
                if s == 0 and zz != far_half(way):
                    continue
                d = (4 - s) if way == CW else (s - 4)
                own = part.at[d % NY, zz, pl.ds(c * width, width)]
                if s == 2:
                    value = own[...].astype(F32) + rs_in[way, 1, zz, c].astype(F32)
                    if zz == far_half(way):
                        value = value + rs_in[way, 0, zz, c].astype(F32)
                    own[...] = value.astype(BF16)
                relay = at_y((2, 1, 2, 1)[s] * (1 if way == CW else -1))
                send(own, rs_in.at[way, s, zz, c], rs_sem.at[s, zz, c], relay)

    def rs_sum(c, zz):
        own = part[0, zz, pl.ds(c * width, width)].astype(F32)
        for s in (2, 3) if (c, zz) in relayed else (3,):
            wait(2 * width, rs_sem.at[s, zz, c])
            for way in (CW, CCW):
                own = own + rs_in[way, s, zz, c].astype(F32)
        return own

    def rs_across(c):
        z_send[c] = rs_sum(c, OTHER).astype(BF16)
        send(z_send.at[c], z_in.at[c], z_sem.at[c], across)

    last = NC - 1
    half = width // 2

    def last_piece(d):
        return part.at[d % NY, OWN, pl.ds(last * width, width)]

    def zf_send(d):
        send(part.at[d % NY, OTHER, pl.ds(last * width, width)], zf_in.at[d % NY], zf_sem.at[abs(d)], across)

    def zf_add(*ds):
        wait(len(ds) * width, zf_sem.at[abs(ds[0])])
        for d in ds:
            own = last_piece(d)
            own[...] = (own[...].astype(F32) + zf_in[d % NY].astype(F32)).astype(BF16)

    def zf_rs(s):
        zf_add(*((4,) if s == 0 else (4 - s, s - 4)))
        if s == 2:
            wait(width, rs_sem.at[0, OWN, last])
            wait(2 * width, rs_sem.at[1, OWN, last])
        for way in (CW, CCW):
            d = (4 - s) if way == CW else (s - 4)
            relay = at_y((2, 1, 2, 1)[s] * (1 if way == CW else -1))
            inbox = rs_in.at[way, :, OWN, last]
            halved = pl.ds(way * half, half)
            if s == 2:
                own = last_piece(d).at[halved]
                own[...] = (own[...].astype(F32) + inbox[0, halved].astype(F32)).astype(BF16)
                own = last_piece(d)
                own[...] = (own[...].astype(F32) + inbox[1].astype(F32)).astype(BF16)
            rows = halved if s == 0 else pl.ds(0, width)
            send(last_piece(d).at[rows], inbox.at[s, rows], rs_sem.at[s, OWN, last], relay)

    def adam(c):
        if "state" not in waited:
            waited.add("state")
            loaded(NY + 2, state)
        columns = pl.ds(c * width, width)
        if c == last:
            zf_add(0)
        own = rs_sum(c, OWN)
        if c != last:
            wait(width, z_sem.at[c])
            own = own + z_in[c].astype(F32)
        gradient = own.T
        new_one = 0.9 * m_v[:, columns] + 0.1 * gradient
        new_two = 0.95 * s_v[:, columns] + 0.05 * gradient * gradient
        power = jnp.full(new_one.shape, step[0] + 1, jnp.int32).astype(F32)
        corr_one = 1.0 - jnp.exp(power * math.log(0.9))
        corr_two = 1.0 - jnp.exp(power * math.log(0.95))
        updated = w_v[:, columns] - 0.01 * (new_one / corr_one) / (jnp.sqrt(new_two / corr_two) + 1e-08)
        mate_send[c] = updated.astype(BF16)
        send(mate_send.at[c], mate_in.at[c], mate_sem.at[c], mate(mask))
        w_v[:, columns] = updated
        first_v[0, :, columns] = new_one
        second_v[0, :, columns] = new_two

    mine = lax.rem(r // mask, 2)

    def rows_of(d, c, zz, start, rows):
        return weights.at[d % NY, c // 2, pl.ds(zz * depth + start, rows), pl.ds((c % 2) * width, width)]

    def ring(d, c, zz):
        if c in shared:
            return rows_of(d, c, zz, pl.multiple_of(mine * (depth // 2), depth // 2), depth // 2)
        return rows_of(d, c, zz, 0, depth)

    def mix(c):
        columns = pl.ds(c * width, width)
        wait(depth, mate_sem.at[c])
        mixed = 0.5 * (w_v[:, columns] + mate_in[c].astype(F32))
        mixed_v[0, :, columns] = mixed
        rows_of(0, c, OWN, 0, depth)[...] = mixed.astype(BF16)
        send(ring(0, c, OWN), ring(0, c, OTHER), gz_sem.at[c], across)

    def once(key, rows, sem):
        if key not in waited:
            waited.add(key)
            wait(rows, sem)

    def ag_wait(d, c, zz):
        rows = depth // 2 if c in shared else depth
        if d != 0:
            once((abs(d), c, zz), rows if d == 4 else 2 * rows, ag_sem.at[abs(d) - 1, zz, c])
        elif zz == OTHER:
            once((0, c, zz), rows, gz_sem.at[c])

    def ag_send(have, there, way, c, zz):
        device = at_y(abs(have - there) * (1 if way == CW else -1))
        send(ring(have, c, zz), ring(there, c, zz), ag_sem.at[abs(there) - 1, zz, c], device)

    def ag(s, *pieces):
        for c, zz in pieces:
            for way in (CW, CCW):
                if s == 4 and zz == far_half(way):
                    continue
                have, there = (1 - s, -s) if way == CW else (s - 1, s)
                ag_wait(have, c, zz)
                ag_send(have, there, way, c, zz)

    def skip(stage, *pieces):
        for c, zz in pieces:
            for way in (CW, CCW):
                sign = -1 if way == CW else 1
                if stage == 1:
                    ag_wait(0, c, zz)
                    ag_send(0, 2 * sign, way, c, zz)
                else:
                    ag_wait(2 * sign, c, zz)
                    if zz != far_half(way):
                        ag_send(2 * sign, 4 * sign, way, c, zz)
            for way in (CW, CCW):
                sign = -1 if way == CW else 1
                if stage == 1:
                    ag_send(0, sign, way, c, zz)
                else:
                    ag_send(2 * sign, 3 * sign, way, c, zz)

    def fwd(c, d, zz):
        ag_wait(d, c, zz)
        there = ring(d, c, zz)
        send(there, there, fwd_sem.at[c // 2, abs(d)], mate(mask))

    def multiply(pair, *ds):
        for d in ds:
            for c in (2 * pair, 2 * pair + 1):
                for zz in (OWN, OTHER):
                    ag_wait(d, c, zz)
            passed = sum(c in shared for c in (2 * pair, 2 * pair + 1)) * (1, 4, 4, 4, 2)[abs(d)]
            if passed:
                once(("passed", pair, abs(d)), passed * (depth // 2), fwd_sem.at[pair, abs(d)])
            term = jnp.dot(x[d % NY], weights[d % NY, pair], preferred_element_type=F32)
            if d == 0:
                total[pair] = term
            elif d != 4:
                total[pair] += term
            else:
                keys[0, :, pl.ds(pair * 2 * width, 2 * width)] = (total[pair] + term).astype(BF16)

    w0, o0, w1, o1 = (0, OWN), (0, OTHER), (1, OWN), (1, OTHER)
    w2, o2, w3, o3 = (2, OWN), (2, OTHER), (3, OWN), (3, OTHER)

    prepare()
    if mask == 1:
        partial(4)
        enter()
        rs(0, o0, o1, o2)
        partial(-3)
        rs(0, w0, w2)
        partial(2)
        rs(0, w1)
        partial(3)
        zf_send(4)
        zf_send(-3)
        partial(-2)
        zf_send(3)
        partial(0)
        zf_send(-2)
        partial(1)
        rs(1, o0)
        partial(-1)
        rs(1, o1, w0)
        zf_send(2)
        zf_send(-1)
        zf_send(0)
        rs(1, o2, w2)
        zf_send(1)
        rs(1, w1)
        rs(2, o0, o1, w0)
        zf_rs(0)
        rs(2, o2, w2, w1)
        rs(3, o0)
        zf_rs(1)
        rs(3, o1, w0, o2, w2, w1)
        rs_across(0)
        zf_rs(2)
        rs_across(1)
        zf_rs(3)
        rs_across(2)
        adam(3)
        adam(0)
        mix(3)
        skip(1, w3)
        adam(1)
        mix(0)
        ag(1, w0)
        adam(2)
        mix(1)
        ag(1, w1)
        mix(2)
        skip(1, w2)
        fwd(3, -1, OWN)
        fwd(3, 1, OWN)
        ag(2, w0)
        skip(2, w3)
        fwd(3, 2, OWN)
        fwd(3, -2, OWN)
        fwd(0, -1, OWN)
        fwd(0, 1, OWN)
        fwd(1, -1, OWN)
        ag(2, w1)
        fwd(1, 1, OWN)
        skip(1, o3)
        fwd(3, 0, OTHER)
        skip(1, o0)
        fwd(0, 0, OTHER)
        fwd(2, -1, OWN)
        fwd(2, 1, OWN)
        ag(3, w0)
        fwd(0, -2, OWN)
        fwd(3, 3, OWN)
        fwd(1, 0, OTHER)
        skip(1, o1)
        fwd(1, 2, OWN)
        fwd(3, -3, OWN)
        fwd(2, 2, OWN)
        fwd(0, 2, OWN)
        fwd(1, -2, OWN)
        fwd(3, 4, OWN)
        multiply(0, 0)
        skip(1, o2)
        fwd(2, 0, OTHER)
        ag(3, w1)
        fwd(3, 1, OTHER)
        fwd(3, -1, OTHER)
        fwd(2, -2, OWN)
        skip(2, w2)
        fwd(3, 2, OTHER)
        multiply(1, 0)
        skip(2, o3)
        fwd(3, -2, OTHER)
        fwd(0, 1, OTHER)
        fwd(0, -3, OWN)
        skip(2, o0)
        fwd(0, 2, OTHER)
        fwd(0, 3, OWN)
        ag(4, w0)
        fwd(0, -2, OTHER)
        fwd(0, -1, OTHER)
        fwd(1, 1, OTHER)
        fwd(1, -1, OTHER)
        fwd(1, 2, OTHER)
        fwd(1, -2, OTHER)
        skip(2, o1)
        multiply(0, -1)
        fwd(2, 1, OTHER)
        multiply(0, 1, 2)
        fwd(2, -2, OTHER)
        fwd(1, -3, OWN)
        fwd(1, 3, OWN)
        skip(2, o2)
        multiply(0, -2)
        fwd(2, 2, OTHER)
        ag(4, w1)
        fwd(2, -3, OWN)
        fwd(2, -1, OTHER)
        fwd(2, 3, OWN)
        fwd(3, -3, OTHER)
        fwd(3, 3, OTHER)
        fwd(2, 4, OWN)
        fwd(0, -3, OTHER)
        multiply(1, 2, -1, 1)
        fwd(1, -3, OTHER)
        multiply(1, -2)
        fwd(0, 4, OWN)
        fwd(3, 4, OTHER)
        fwd(0, 3, OTHER)
        fwd(0, 4, OTHER)
        fwd(1, 3, OTHER)
        fwd(2, -3, OTHER)
        fwd(1, 4, OTHER)
        fwd(1, 4, OWN)
        multiply(0, -3)
        fwd(2, 3, OTHER)
        multiply(0, 3)
        fwd(2, 4, OTHER)
        multiply(0, 4)
        multiply(1, 3, -3, 4)
    elif mask in (2, 4):
        partial(4)
        enter()
        rs(0, o1, w1, w0, o2, o0)
        partial(-3)
        rs(0, w2)
        partial(3)
        partial(-1)
        zf_send(3)
        partial(-2)
        partial(0)
        partial(2)
        rs(1, o1, w1)
        zf_send(2)
        zf_send(-1)
        zf_send(-2)
        zf_send(-3)
        rs(1, o2, w0)
        zf_send(0)
        zf_send(4)
        partial(1)
        rs(1, o0, w2)
        zf_send(1)
        rs(2, o1, w1, o2, w0, o0, w2)
        rs(3, o1, w1, o2, w0, o0, w2)
        zf_rs(1)
        rs_across(1)
        rs_across(2)
        zf_rs(0)
        rs_across(0)
        zf_rs(3)
        zf_rs(2)
        adam(1)
        adam(2)
        adam(0)
        mix(1)
        ag(1, w1)
        mix(2)
        ag(1, w2)
        adam(3)
        mix(0)
        ag(1, w0)
        fwd(1, -1, OWN)
        ag(2, w1)
        fwd(1, 1, OWN)
        ag(2, w2)
        fwd(2, 1, OWN)
        fwd(2, -1, OWN)
        mix(3)
        ag(1, w3)
        fwd(0, 1, OWN)
        ag(2, w0)
        fwd(0, -1, OWN)
        skip(1, o1)
        fwd(1, 0, OTHER)
        ag(3, w1)
        fwd(1, 2, OWN)
        fwd(1, -2, OWN)
        skip(1, o2)
        fwd(2, 0, OTHER)
        ag(3, w2)
        fwd(2, 2, OWN)
        fwd(2, -2, OWN)
        skip(1, o0)
        ag(2, w3)
        fwd(0, 0, OTHER)
        ag(3, w0)
        fwd(0, -2, OWN)
        fwd(0, 2, OWN)
        fwd(1, -1, OTHER)
        fwd(1, 1, OTHER)
        fwd(1, -3, OWN)
        fwd(1, 3, OWN)
        ag(4, w1)
        skip(2, o1)
        fwd(1, -2, OTHER)
        fwd(1, 2, OTHER)
        fwd(2, 1, OTHER)
        fwd(2, -1, OTHER)
        ag(4, w2)
        skip(1, o3)
        fwd(2, -3, OWN)
        fwd(2, 2, OTHER)
        multiply(0, 0)
        fwd(2, 3, OWN)
        fwd(2, -2, OTHER)
        multiply(1, 0)
        skip(2, o2)
        fwd(0, -1, OTHER)
        fwd(0, 1, OTHER)
        skip(2, o0)
        ag(3, w3)
        fwd(0, 2, OTHER)
        ag(4, w0)
        fwd(0, 3, OWN)
        fwd(0, -3, OWN)
        fwd(0, -2, OTHER)
        fwd(1, 4, OWN)
        fwd(1, -3, OTHER)
        fwd(1, 3, OTHER)
        fwd(2, 4, OWN)
        fwd(1, 4, OTHER)
        multiply(1, 1, -1)
        skip(2, o3)
        multiply(1, -2)
        fwd(2, -3, OTHER)
        fwd(0, -3, OTHER)
        multiply(1, 2)
        multiply(0, 2)
        fwd(2, 3, OTHER)
        multiply(0, -1, 1)
        ag(4, w3)
        fwd(2, 4, OTHER)
        fwd(0, 4, OWN)
        multiply(0, -2)
        fwd(0, 3, OTHER)
        fwd(0, 4, OTHER)
        multiply(1, -3, 3, 4)
        multiply(0, -3, 3, 4)
    else:
        partial(4)
        enter()
        rs(0, o2, o0)
        partial(0)
        rs(0, w1)
        partial(-1)
        zf_send(-1)
        partial(-2)
        zf_send(-2)
        rs(0, o1)
        zf_send(0)
        partial(2)
        zf_send(2)
        rs(0, w0)
        partial(-3)
        zf_send(-3)
        partial(3)
        zf_send(3)
        rs(1, o2)
        rs(0, w2)
        zf_send(4)
        partial(1)
        rs(1, o0)
        zf_send(1)
        rs(1, w1, o1, w0)
        rs(2, o2)
        rs(1, w2)
        rs(2, o0, w1, o1, w0)
        rs(3, o2)
        rs(2, w2)
        rs(3, o0, w1, o1, w0)
        zf_rs(1)
        rs_across(2)
        rs(3, w2)
        zf_rs(0)
        rs_across(0)
        zf_rs(3)
        rs_across(1)
        zf_rs(2)
        adam(2)
        adam(0)
        adam(1)
        mix(2)
        ag(1, w2)
        adam(3)
        mix(0)
        ag(1, w0)
        mix(1)
        ag(1, w1)
        ag(2, w2)
        fwd(2, -1, OWN)
        fwd(2, 1, OWN)
        mix(3)
        ag(1, w3)
        ag(2, w0)
        fwd(0, -1, OWN)
        fwd(0, 1, OWN)
        ag(2, w1)
        fwd(1, 1, OWN)
        fwd(1, -1, OWN)
        skip(1, o2)
        ag(3, w2)
        fwd(2, 0, OTHER)
        fwd(2, -2, OWN)
        fwd(2, 2, OWN)
        skip(1, o0)
        fwd(0, 0, OTHER)
        ag(2, w3)
        ag(3, w0)
        fwd(0, -2, OWN)
        fwd(0, 2, OWN)
        skip(1, o1)
        ag(3, w1)
        fwd(1, -2, OWN)
        fwd(1, 0, OTHER)
        fwd(1, 2, OWN)
        fwd(2, 1, OTHER)
        fwd(2, -1, OTHER)
        ag(4, w2)
        fwd(2, 3, OWN)
        fwd(2, -3, OWN)
        skip(2, o2)
        fwd(2, 2, OTHER)
        fwd(2, -2, OTHER)
        skip(1, o3)
        multiply(1, 0)
        fwd(0, 1, OTHER)
        fwd(0, -1, OTHER)
        skip(2, o0)
        fwd(0, 2, OTHER)
        ag(3, w3)
        fwd(0, -2, OTHER)
        ag(4, w0)
        fwd(0, -3, OWN)
        multiply(0, 0)
        fwd(0, 3, OWN)
        fwd(1, -1, OTHER)
        fwd(1, 1, OTHER)
        ag(4, w1)
        fwd(1, -3, OWN)
        fwd(1, 3, OWN)
        fwd(1, 2, OTHER)
        skip(2, o1)
        fwd(1, -2, OTHER)
        fwd(2, 4, OWN)
        fwd(2, -3, OTHER)
        fwd(2, 3, OTHER)
        fwd(2, 4, OTHER)
        multiply(1, -1)
        fwd(0, -3, OTHER)
        skip(2, o3)
        multiply(1, 2, 1)
        ag(4, w3)
        multiply(0, -1, 1)
        fwd(0, 4, OWN)
        multiply(1, -2)
        fwd(0, 3, OTHER)
        fwd(1, 4, OWN)
        fwd(0, 4, OTHER)
        fwd(1, -3, OTHER)
        multiply(0, -2, 2)
        fwd(1, 3, OTHER)
        fwd(1, 4, OTHER)
        multiply(1, -3, 3, 4)
        multiply(0, 3, -3, 4)

    wait(sum(sent), send_sem.at[0])


def store(*refs):
    count = len(refs) // 2
    sem = refs[-1]
    copies = [pltpu.make_async_copy(refs[i], refs[count + i], sem.at[i]) for i in range(count)]
    for copy in copies:
        copy.start()
    for copy in copies:
        copy.wait()


def on_device(inputs, key_grads, token_ids, step, master, first_moment, second_moment):
    tokens, features = inputs.shape[1:]
    depth, columns = master.shape[1:]
    width = columns // NC
    hbm = pl.BlockSpec(memory_space=pltpu.HBM)
    vmem = pl.BlockSpec(memory_space=pltpu.VMEM)
    any_space = pl.BlockSpec(memory_space=pl.ANY)
    dma = pltpu.SemaphoreType.DMA
    shapes = [(master.shape, F32)] * 3 + [((1, tokens, columns), BF16)]

    def with_partner(bit, *operands):
        mask = PARTNERS[bit]
        shared = SHARED[bit]
        results = pl.pallas_call(
            functools.partial(kernel, mask, shared),
            out_shape=[pltpu.VMEM(shape, dtype) for shape, dtype in shapes],
            in_specs=[hbm] * 3 + [pl.BlockSpec(memory_space=pltpu.SMEM)] + [hbm] * 3,
            out_specs=[vmem] * 4,
            scratch_shapes=[
                pltpu.VMEM((NY, tokens, 2 * depth), BF16),
                pltpu.VMEM((tokens, columns), BF16),
                pltpu.VMEM((1, tokens), jnp.int32),
                pltpu.VMEM((columns, tokens), BF16),
                pltpu.VMEM((NY, 2, columns, depth), BF16),
                pltpu.VMEM((2, 4, 2, NC, width, depth), BF16),
                pltpu.VMEM((NY, width, depth), BF16),
                pltpu.VMEM((NY, NC // 2, 2 * depth, 2 * width), BF16),
                pltpu.VMEM((NC // 2, tokens, 2 * width), F32),
                pltpu.VMEM((NC, width, depth), BF16),
                pltpu.VMEM((NC, width, depth), BF16),
                pltpu.VMEM((NC, depth, width), BF16),
                pltpu.VMEM((NC, depth, width), BF16),
                pltpu.VMEM((3, depth, columns), F32),
                pltpu.VMEM((NC * 32 * depth, depth), BF16),
                dma((NY + 3,)),
                dma((1,)),
                dma((4, 2, NC)),
                dma((4, 2, NC)),
                dma((NC,)),
                dma((NC,)),
                dma((NC,)),
                dma((5,)),
                dma((NC // 2, 5)),
            ],
            compiler_params=pltpu.CompilerParams(
                collective_id=bit, has_side_effects=True, vmem_limit_bytes=58 * 2**20
            ),
            cost_estimate=pl.CostEstimate(
                flops=4 * tokens * features * columns, bytes_accessed=5 * 2**20, transcendentals=0
            ),
            name="grad_adam_keys",
        )(*operands)
        results = [pltpu.with_memory_space_constraint(result, pltpu.VMEM) for result in results]
        return pl.pallas_call(
            store,
            out_shape=[jax.ShapeDtypeStruct(shape, dtype) for shape, dtype in shapes],
            in_specs=[any_space] * 4,
            out_specs=[any_space] * 4,
            scratch_shapes=[dma((4,))],
            name="store_results",
        )(*results)

    branches = [functools.partial(with_partner, bit) for bit in range(len(PARTNERS))]
    return lax.switch(
        lax.rem(step, len(PARTNERS)), branches,
        inputs, key_grads, token_ids, step.reshape(1), master, first_moment, second_moment,
    )


def solution(mesh):
    in_specs = (
        P("rep", "fsdp", None),
        P("rep", "fsdp", None),
        P("rep", "fsdp"),
        P(),
        P("rep", "fsdp", None),
        P("rep", "fsdp", None),
        P("rep", "fsdp", None),
    )
    out_specs = (
        P("rep", "fsdp", None),
        P("rep", "fsdp", None),
        P("rep", "fsdp", None),
        P("rep", "fsdp", None),
    )
    return jax.shard_map(
        on_device, mesh=mesh, in_specs=in_specs, out_specs=out_specs, check_vma=False
    )
```
